256 devices in a mesh: frame: 32 (over z, x_hi, core), band: 8 (over x_lo, y).
Axes of the slice: x: 4 (x_hi: 2, x_lo: 2; x = x_hi * 2 + x_lo), y: 4, z: 8, core: 2. Of those that a mesh axis runs over, the one named last changes fastest.
Arguments:
- frames: bfloat16 [256, 64, 16, 320], P('frame', 'band'), may hold values from -6 to 6
- control: bfloat16 [256, 64, 16, 320], P('frame', 'band'), may hold values from -4 to 4
- conv_first: bfloat16 [3, 3, 320, 320], replicated, may hold values from -0.109375 to 0.109375
- conv_second: bfloat16 [3, 3, 320, 320], replicated, may hold values from -0.109375 to 0.109375
- time_table: float32 [1000, 320], replicated, may hold values from -5 to 5
- step_index: int32 [1], replicated, may hold values from 0 to 999
- norm_gain: float32 [320], replicated, may hold values from 0.5 to 1.5
- w_query: bfloat16 [320, 320], replicated, as said below
- w_key: bfloat16 [320, 320], replicated, as said below
- w_value: bfloat16 [320, 320], replicated, may hold values from -0.3125 to 0.3125
- w_out: bfloat16 [320, 320], replicated, may hold values from -0.3125 to 0.3125
- rel_bias: float32 [8, 33], replicated, may hold values from -4 to 4
- reach: int32 [256], replicated, may hold values from 4 to 16, as said below
Outputs:
- section_out: float32 [256, 64, 16, 320], P('frame', 'band')
The draws below stay inside these ranges and needn't reach their ends.
Inputs may be any that keep to these rules, and one draw needn't show every extreme that they name: Each frame attends within reach[f] frames on the loop; the first and last frame of each aligned block of 8 frames have reach 16. `w_query`: projection into 8 heads. `w_key`: projection into 8 heads.
All inputs are finite; a program needn't handle non-finite values.
Results may differ from the reference program's by a relative error of at most 0.012.
The reference program's roundings to bfloat16 on the way (of `merged`, `activated`, `normed`, `weights` and `attended`) count: a program that leaves them out, or rounds other values in their place, can miss the bound.
Values may be sent and summed in bfloat16 or wider, within the bound.
No kernel may reach another device: no remote copies, remote signals or barrier semaphores. Data moves between devices by JAX's collectives and lax.ppermute only.
A program may use at most 128 MiB of HBM per device.

```python
import jax
import jax.numpy as jnp
from jax import lax

C = 320
HEADS = 8
F_DEV = 8
COLS = 16
STEPS = 1000
REACH = 16
FRAMES = 256
ROWS = 64


def scaled_columns(key, spread):
    base = jax.random.normal(jax.random.fold_in(key, 1), (C, C), jnp.float32) * C ** (-0.5)
    factor = jnp.exp(jax.random.uniform(jax.random.fold_in(key, 2), (HEADS,), jnp.float32) * spread)
    return (base * jnp.repeat(factor, C // HEADS)[None, :]).astype(jnp.bfloat16)


def draw_w_query(key, part):
    key = jax.random.fold_in(key, 11)
    return scaled_columns(key, 0.0)


def draw_w_key(key, part):
    key = jax.random.fold_in(key, 12)
    return scaled_columns(key, 0.0)


def draw_reach(key, part):
    key = jax.random.fold_in(key, 13)
    base = jax.random.randint(key, (FRAMES,), 4, REACH + 1, dtype=jnp.int32)
    position = jnp.arange(FRAMES, dtype=jnp.int32) % F_DEV
    edge = (position == 0) | (position == F_DEV - 1)
    return jnp.where(edge, REACH, base).astype(jnp.int32)


def level_of(stream_key, extent, split, smallest, high):
    def one(axis_at, parts):
        heights = jax.random.uniform(jax.random.fold_in(jax.random.fold_in(stream_key, 6), axis_at), (parts,), jnp.float32, smallest / len(split), high / len(split))
        return jnp.repeat(jnp.exp(heights), extent[axis_at] // parts).reshape((-1,) + (1,) * (len(extent) - axis_at - 1))

    level = one(*split[0])
    for cut in split[1:]:
        level = level * one(*cut)
    return level


def scatter_about(rng, dims, scale, limit, pieces=(), kind=jnp.bfloat16):
    factor_of = level_of(rng, dims, pieces, -0.22, 0.18) if pieces else 1.0
    entries = jax.random.normal(rng, dims, jnp.float32) * scale * factor_of
    return jnp.minimum(jnp.maximum(entries, -limit), limit).astype(kind)


def setup_inputs(seed: int = 0) -> dict:
    arg_keys = jax.random.split(jax.random.key(seed), 14)
    frames = scatter_about(arg_keys[0], (FRAMES, ROWS, COLS, C), 1.0, 6.0, ((0, 32), (1, 8)))
    control = scatter_about(arg_keys[1], (FRAMES, ROWS, COLS, C), 0.5, 4.0, ((0, 32), (1, 8)))
    conv_first = scatter_about(arg_keys[2], (3, 3, C, C), (9 * C) ** -0.5, 0.109375)
    conv_second = scatter_about(arg_keys[3], (3, 3, C, C), (9 * C) ** -0.5, 0.109375)
    time_table = scatter_about(arg_keys[4], (STEPS, C), 1.0, 5.0, (), jnp.float32)
    step_index = jax.random.randint(arg_keys[5], (1,), 0, STEPS).astype(jnp.int32)
    norm_gain = jnp.clip(1.0 + 0.1 * jax.random.normal(arg_keys[6], (C,), jnp.float32), 0.5, 1.5)
    w_query = draw_w_query(jax.random.fold_in(arg_keys[13], 71), 0)
    w_key = draw_w_key(jax.random.fold_in(arg_keys[13], 71), 0)
    w_value = scatter_about(arg_keys[9], (C, C), C ** -0.5, 0.3125)
    w_out = scatter_about(arg_keys[10], (C, C), C ** -0.5, 0.3125)
    rel_bias = scatter_about(arg_keys[11], (HEADS, 2 * REACH + 1), 1.0, 4.0, (), jnp.float32)
    reach = draw_reach(jax.random.fold_in(arg_keys[13], 71), 0)
    return {"frames": frames, "control": control, "conv_first": conv_first, "conv_second": conv_second, "time_table": time_table, "step_index": step_index, "norm_gain": norm_gain, "w_query": w_query, "w_key": w_key, "w_value": w_value, "w_out": w_out, "rel_bias": rel_bias, "reach": reach}


def conv_full(field, weight):
    return lax.conv_general_dilated(field.astype(jnp.float32), weight.astype(jnp.float32), (1, 1), ((1, 1), (1, 1)), dimension_numbers=('NHWC', 'HWIO', 'NHWC'), precision=lax.Precision.HIGHEST)

def attend(query, key, value, q_frames, k_frames, reach_q, rel_bias, total):
    heads = rel_bias.shape[0]
    span = (rel_bias.shape[1] - 1) // 2
    fq, pix, chans = query.shape
    fk = key.shape[0]
    dh = chans // heads
    q4 = query.reshape(fq, pix, heads, dh).astype(jnp.float32)
    k4 = key.reshape(fk, pix, heads, dh).astype(jnp.float32)
    v4 = value.reshape(fk, pix, heads, dh).astype(jnp.float32)
    scores = jnp.einsum('iphd,jphd->phij', q4, k4) * dh ** (-0.5)
    delta = ((k_frames[None, :] - q_frames[:, None] + total // 2) % total - total // 2).astype(jnp.int32)
    table = (delta[:, :, None] + span == jnp.arange(2 * span + 1, dtype=jnp.int32)[None, None, :]).astype(jnp.float32)
    bias = jnp.einsum('ijs,hs->hij', table, rel_bias, precision=lax.Precision.HIGHEST)
    allowed = jnp.abs(delta) <= reach_q[:, None]
    scores = jnp.where(allowed[None, None], scores + bias[None], -jnp.inf)
    top = lax.optimization_barrier(jnp.max(scores, axis=-1, keepdims=True))
    expo = jnp.exp(scores - top)
    weights = (expo / lax.optimization_barrier(jnp.sum(expo, axis=-1, keepdims=True))).astype(jnp.bfloat16)
    out = jnp.einsum('phij,jphd->iphd', weights.astype(jnp.float32), v4)
    return out.astype(jnp.bfloat16).reshape(fq, pix, chans)

def reference(frames, control, conv_first, conv_second, time_table, step_index, norm_gain, w_query, w_key, w_value, w_out, rel_bias, reach):
    total, rows, cols, chans = frames.shape
    pixels = rows * cols
    blocks = total // F_DEV
    picker = (jnp.arange(time_table.shape[0], dtype=jnp.int32) == step_index[0]).astype(jnp.float32)
    embed = jnp.dot(picker, time_table, precision=lax.Precision.HIGHEST)

    def front(pair):
        xin, cin = pair
        merged = (xin.astype(jnp.float32) + cin.astype(jnp.float32)).astype(jnp.bfloat16)
        activated = jax.nn.silu(conv_full(merged, conv_first) + embed).astype(jnp.bfloat16)
        block_out = merged.astype(jnp.float32) + conv_full(activated, conv_second)
        flat = block_out.reshape(F_DEV * pixels, chans)
        centre = flat - lax.optimization_barrier(jnp.mean(flat, axis=1, keepdims=True))
        normed = (centre * lax.rsqrt(lax.optimization_barrier(jnp.mean(centre * centre, axis=1, keepdims=True)) + 1e-05) * norm_gain).astype(jnp.bfloat16)
        query = jnp.dot(normed, w_query, preferred_element_type=jnp.float32).astype(jnp.bfloat16)
        key = jnp.dot(normed, w_key, preferred_element_type=jnp.float32).astype(jnp.bfloat16)
        value = jnp.dot(normed, w_value, preferred_element_type=jnp.float32).astype(jnp.bfloat16)
        return (flat.reshape(F_DEV, pixels, chans), query.reshape(F_DEV, pixels, chans), key.reshape(F_DEV, pixels, chans), value.reshape(F_DEV, pixels, chans))
    shaped = (frames.reshape(blocks, F_DEV, rows, cols, chans), control.reshape(blocks, F_DEV, rows, cols, chans))
    block_out, query, key, value = lax.map(front, shaped)
    key = key.reshape(total, pixels, chans)
    value = value.reshape(total, pixels, chans)
    hops = -(-REACH // F_DEV)

    def back(item):
        index, q_blk, r_blk = item
        base = index * F_DEV
        picks = ((base + jnp.arange(-hops * F_DEV, (hops + 1) * F_DEV, dtype=jnp.int32)) % total).astype(jnp.int32)
        q_frames = (base + jnp.arange(F_DEV, dtype=jnp.int32)).astype(jnp.int32)
        reach_q = lax.dynamic_slice_in_dim(reach, base.astype(jnp.int32), F_DEV)
        attended = attend(q_blk, jnp.take(key, picks, axis=0), jnp.take(value, picks, axis=0), q_frames, picks, reach_q, rel_bias, total)
        mixed = jnp.dot(attended.reshape(F_DEV * pixels, chans), w_out, preferred_element_type=jnp.float32)
        return r_blk.reshape(F_DEV * pixels, chans) + mixed
    result = lax.map(back, (jnp.arange(blocks, dtype=jnp.int32), query, block_out))
    return result.reshape(total, rows, cols, chans)
```

```python
import functools
import math

import jax
import jax.numpy as jnp
import numpy as np
from jax import lax
from jax.experimental import pallas as pl
from jax.experimental.pallas import tpu as pltpu
from jax.sharding import PartitionSpec as P

BF = jnp.bfloat16
F32 = jnp.float32
GROUP = 4
VMEM_BYTES = 52 * 1024 * 1024


def tapped(dst, row, tap, value):
    dst[row, :, tap * 256 : tap * 256 + 256] = value[:, :256]
    dst[row, :, 768 + tap * 64 : 832 + tap * 64] = value[:, 256:]


def arrange(dst, weight):
    for dy in range(3):
        for dx in range(3):
            w = weight[dy, dx]
            top = slice(dy * 256, dy * 256 + 256)
            low = slice(768 + dy * 64, 832 + dy * 64)
            left = slice(dx * 256, dx * 256 + 256)
            right = slice(768 + dx * 64, 832 + dx * 64)
            dst[top, left] = w[:256, :256]
            dst[top, right] = w[:256, 256:]
            dst[low, left] = w[256:, :256]
            dst[low, right] = w[256:, 256:]


def combine(prod, rows):
    def shifted(a, b, c):
        gap = jnp.zeros((8, a.shape[1]), F32)
        return (
            b
            + jnp.concatenate([gap, a[:-8]], axis=0)
            + jnp.concatenate([c[8:], gap], axis=0)
        )

    main = shifted(prod[rows, 0:256], prod[rows, 256:512], prod[rows, 512:768])
    rest = shifted(prod[rows, 768:832], prod[rows, 832:896], prod[rows, 896:960])
    return jnp.concatenate([main, rest], axis=1)


def conv_kernel(
    meta, frames, control, low, high, first, second, table, gain,
    out0, out1, out2, out3, flat,
    merged, taps1, taps2, wide1, wide2, prod, normed,
):
    me = meta[0]

    def put(row, f, value):
        value = value.astype(BF).astype(F32)
        rest = jnp.concatenate([value[:, 256:], jnp.zeros((16, 64), F32)], axis=1)
        for j, part in enumerate((value[:, :128], value[:, 128:256], rest)):
            merged[j, row, pl.ds(f, 16, stride=8), :] = part

    def taken(row):
        return jnp.concatenate([merged[0, row], merged[1, row], merged[2, row, :, :64]], axis=1)

    for f in range(8):
        for y in range(8):
            put(y + 2, f, frames[f, y].astype(F32) + control[f, y].astype(F32))
        for y in range(2):
            put(y, f, low[f, y].astype(F32))
            put(y + 10, f, high[f, y].astype(F32))
    for m in range(12):
        value = taken(m).astype(BF)
        for dy in range(3):
            if 0 <= m - dy < 10:
                tapped(taps1, m - dy, dy, value)
    arrange(wide1, first)
    arrange(wide2, second)
    embed = table[pl.ds(meta[3], 1), :]
    for part in range(2):
        prod[...] = jnp.dot(
            taps1[part * 5 : part * 5 + 5].reshape(640, 960), wide1[...],
            preferred_element_type=F32,
        )
        for i in range(5):
            row = part * 5 + i
            t = combine(prod, slice(i * 128, i * 128 + 128)) + embed
            act = t * (0.5 * jnp.tanh(0.5 * t) + 0.5)
            if row == 0:
                act = jnp.where(meta[1] == 1, 0.0, act)
            if row == 9:
                act = jnp.where(meta[2] == 1, 0.0, act)
            act = act.astype(BF)
            for dy in range(3):
                if 0 <= row - dy < 8:
                    tapped(taps2, row - dy, dy, act)
    for part in range(2):
        prod[0:512, :] = jnp.dot(
            taps2[part * 4 : part * 4 + 4].reshape(512, 960), wide2[...],
            preferred_element_type=F32,
        )
        for i in range(4):
            y = part * 4 + i
            block = combine(prod, slice(i * 128, i * 128 + 128)) + taken(y + 2)
            flat[y] = block
            mean = jnp.sum(block, axis=1, keepdims=True) * (1.0 / 320)
            centre = block - mean
            var = jnp.sum(centre * centre, axis=1, keepdims=True) * (1.0 / 320)
            normed[y] = (centre * lax.rsqrt(var + 1e-5) * gain[...]).astype(BF)
    for k, out in enumerate((out0, out1, out2, out3)):
        out[...] = normed[pl.ds(2 * (me ^ k), 2)].reshape(256, 320)


def attend_kernel(
    meta, own0, own1, own2, own3, halo0, halo1, halo2, halo3, wq, wk, wv, bias,
    out0, out1, out2, out3,
    field, wide, query, key, value, back,
):
    me = meta[0]
    for at, w in enumerate((wq, wk, wv)):
        wide[:, at * 256 : at * 256 + 256] = w[:, :256]
        wide[:, 768 + at * 64 : 832 + at * 64] = w[:, 256:]
    for k, own in enumerate((own0, own1, own2, own3)):
        at = pl.multiple_of(16 + 8 * (me ^ k), 8)
        field[:, pl.ds(at, 8), :] = own[...].astype(F32).reshape(32, 8, 320)
    for k, halo in enumerate((halo0, halo1, halo2, halo3)):
        block = me ^ k
        at = pl.multiple_of(jnp.where(block >= 2, 8 * block - 16, 48 + 8 * block), 8)
        field[:, pl.ds(at, 8), :] = halo[...].astype(F32).reshape(32, 8, 320)

    def project(lo, hi, with_query):
        n = hi - lo
        x = field[:, lo:hi, :].reshape(32 * n, 320).astype(BF)
        out = jnp.dot(x, wide[...], preferred_element_type=F32).astype(BF)
        if with_query:
            query[:, :, 0:256] = out[:, 0:256].reshape(32, n, 256)
            query[:, :, 256:320] = out[:, 768:832].reshape(32, n, 64)
        key[:, lo:hi, 0:256] = out[:, 256:512].reshape(32, n, 256)
        key[:, lo:hi, 256:320] = out[:, 832:896].reshape(32, n, 64)
        value[:, lo:hi, 0:256] = out[:, 512:768].reshape(32, n, 256)
        value[:, lo:hi, 256:320] = out[:, 896:960].reshape(32, n, 64)

    project(16, 48, True)
    project(0, 16, False)
    project(48, 64, False)

    lane = lax.broadcasted_iota(jnp.int32, (1, 1, 256), 2)
    head = lax.broadcasted_iota(jnp.int32, (6, 1, 1), 0)
    mask6 = (lane >= head * 40) & (lane < head * 40 + 40)
    lane = lax.broadcasted_iota(jnp.int32, (1, 1, 192), 2)
    head = lax.broadcasted_iota(jnp.int32, (2, 1, 1), 0)
    mask2 = (lane >= 112 + head * 40) & (lane < 152 + head * 40)
    ones6 = mask6.astype(F32)
    ones2 = mask2.astype(F32)
    spread6 = ones6.astype(BF)
    spread2 = ones2.astype(BF)
    scale = 40.0 ** -0.5 / math.log(2.0)
    across = (((1,), (1,)), ((), ()))

    def pixel(p):
        q = query[p]
        k = key[p]
        v = value[p]
        q6 = (q[None, :, 0:256] * spread6).reshape(192, 256)
        q2 = (q[None, :, 128:320] * spread2).reshape(64, 192)
        s = jnp.concatenate(
            [
                lax.dot_general(q6, k[:, 0:256], across, preferred_element_type=F32),
                lax.dot_general(q2, k[:, 128:320], across, preferred_element_type=F32),
            ],
            axis=0,
        )
        s = s * scale + bias[...]
        e = jnp.exp2(s - jnp.max(s, axis=1, keepdims=True))
        w = (e / jnp.sum(e, axis=1, keepdims=True)).astype(BF)
        o6 = jnp.dot(w[:192], v[:, 0:256], preferred_element_type=F32)
        o2 = jnp.dot(w[192:], v[:, 128:320], preferred_element_type=F32)
        a6 = jnp.sum(o6.reshape(6, 32, 256) * ones6, axis=0)
        a2 = jnp.sum(o2.reshape(2, 32, 192) * ones2, axis=0)
        att = jnp.concatenate(
            [a6[:, 0:128], a6[:, 128:256] + a2[:, 0:128], a2[:, 128:192]], axis=1
        )
        for b in range(4):
            back[b, p] = att[8 * b : 8 * b + 8]

    def some(i, carry):
        for j in range(4):
            pixel(i * 4 + j)
        return carry

    lax.fori_loop(0, 8, some, 0)
    for k, out in enumerate((out0, out1, out2, out3)):
        out[...] = back[me ^ k].reshape(256, 320).astype(BF)


def final_kernel(meta, a0, a1, a2, a3, w_out, flat, out, total):
    k = pl.program_id(0)
    for at, a in enumerate((a0, a1, a2, a3)):

        @pl.when(k == at)
        def _():
            mixed = jnp.dot(a[...], w_out[...], preferred_element_type=F32)
            mixed = flat[...].reshape(256, 320) + mixed
            total[0] = mixed[:, :128]
            total[1] = mixed[:, 128:256]
            total[2, :, :64] = mixed[:, 256:]

    for f in range(8):
        for y in range(2):
            for j, width in enumerate((128, 128, 64)):
                part = total[j, pl.ds(y * 128 + f, 16, stride=8), :]
                out[f, y, :, j * 128 : j * 128 + width] = part[:, :width]


def shards(
    frames, control, conv_first, conv_second, time_table, step_index, norm_gain,
    w_query, w_key, w_value, w_out, rel_bias, reach,
):
    count = lax.axis_size("frame")
    bands = lax.axis_size("band")
    planes = count // GROUP
    place = lax.axis_index("frame")
    band = lax.axis_index("band")
    me = place % GROUP
    step = step_index[0]
    meta = jnp.stack(
        [me, (band == 0).astype(jnp.int32), (band == bands - 1).astype(jnp.int32), step % 8, step // 8]
    ).astype(jnp.int32)

    up = [(i, i + 1) for i in range(bands - 1)]
    down = [(i + 1, i) for i in range(bands - 1)]

    def edge(rows):
        return (frames[:, rows].astype(F32) + control[:, rows].astype(F32)).astype(BF)

    low = lax.ppermute(edge(slice(6, 8)), "band", up)
    high = lax.ppermute(edge(slice(0, 2)), "band", down)

    delta = np.arange(64)[None, :] - 16 - np.arange(32)[:, None]
    picks = (delta[:, :, None] + 16 == np.arange(33)[None, None, :]).astype(np.float32)
    bias = jnp.einsum("hs,ijs->hij", rel_bias, picks, precision=lax.Precision.HIGHEST)
    reach_q = lax.dynamic_slice_in_dim(reach, (place // GROUP) * 32, 32)
    allowed = np.abs(delta) <= reach_q[:, None]
    bias = jnp.where(allowed[None], bias * (1.0 / math.log(2.0)), -jnp.inf).reshape(256, 64)

    whole = pl.BlockSpec(memory_space=pltpu.VMEM)
    smem = pl.BlockSpec(memory_space=pltpu.SMEM)
    params = pltpu.CompilerParams(vmem_limit_bytes=VMEM_BYTES)
    piece = jax.ShapeDtypeStruct((256, 320), BF)

    def at(shape):
        return pl.BlockSpec(shape, lambda i, m: (0,) * len(shape))

    n0, n1, n2, n3, flat = pl.pallas_call(
        conv_kernel,
        grid_spec=pltpu.PrefetchScalarGridSpec(
            num_scalar_prefetch=1,
            grid=(1,),
            in_specs=[
                at((8, 8, 16, 320)), at((8, 8, 16, 320)), at((8, 2, 16, 320)), at((8, 2, 16, 320)),
                at((3, 3, 320, 320)), at((3, 3, 320, 320)),
                pl.BlockSpec((8, 320), lambda i, m: (m[4], 0)),
                at((1, 320)),
            ],
            out_specs=[at((256, 320))] * 4 + [at((8, 128, 320))],
            scratch_shapes=[
                pltpu.VMEM((3, 12, 128, 128), F32),
                pltpu.VMEM((10, 128, 960), BF),
                pltpu.VMEM((8, 128, 960), BF),
                pltpu.VMEM((960, 960), BF),
                pltpu.VMEM((960, 960), BF),
                pltpu.VMEM((640, 960), F32),
                pltpu.VMEM((8, 128, 320), BF),
            ],
        ),
        out_shape=[piece] * 4 + [jax.ShapeDtypeStruct((8, 128, 320), F32)],
        compiler_params=params,
        name="conv_block",
    )(meta, frames, control, low, high, conv_first, conv_second, time_table, norm_gain[None])

    pieces = (n0, n1, n2, n3)

    def plane(i, k):
        return (i & ~3) | ((i & 3) ^ k)

    def exchange(x, k):
        return lax.ppermute(x, "frame", [(i, plane(i, k)) for i in range(count)])

    def beside(i, k):
        turn = 1 if i & 2 else -1
        return (((i >> 2) + turn) % planes) * GROUP + ((i & 3) ^ k)

    own = [n0] + [exchange(pieces[k], k) for k in (1, 2, 3)]
    halo = [
        lax.ppermute(pieces[k], "frame", [(i, beside(i, k)) for i in range(count)])
        for k in (0, 1)
    ]
    for k in (2, 3):
        route = [
            (i, (((i >> 2) + (1 if (i ^ k) & 2 else -1)) % planes) * GROUP + (i & 3))
            for i in range(count)
        ]
        halo.append(lax.ppermute(own[k], "frame", route))

    outs = pl.pallas_call(
        attend_kernel,
        in_specs=[smem] + [whole] * 12,
        out_specs=[whole] * 4,
        out_shape=[piece] * 4,
        scratch_shapes=[
            pltpu.VMEM((32, 64, 320), F32),
            pltpu.VMEM((320, 960), BF),
            pltpu.VMEM((32, 32, 320), BF),
            pltpu.VMEM((32, 64, 320), BF),
            pltpu.VMEM((32, 64, 320), BF),
            pltpu.VMEM((4, 32, 8, 320), F32),
        ],
        compiler_params=params,
        name="attend",
    )(meta, *own, *halo, w_query, w_key, w_value, bias)

    back = [outs[0]] + [exchange(outs[k], k) for k in (1, 2, 3)]

    return pl.pallas_call(
        final_kernel,
        grid_spec=pltpu.PrefetchScalarGridSpec(
            num_scalar_prefetch=1,
            grid=(4,),
            in_specs=[at((256, 320))] * 4
            + [at((320, 320)), pl.BlockSpec((2, 128, 320), lambda i, m: (m[0] ^ i, 0, 0))],
            out_specs=pl.BlockSpec((8, 2, 16, 320), lambda i, m: (0, m[0] ^ i, 0, 0)),
            scratch_shapes=[pltpu.VMEM((3, 256, 128), F32)],
        ),
        out_shape=jax.ShapeDtypeStruct((8, 8, 16, 320), F32),
        compiler_params=params,
        name="project_out",
    )(meta, *back, w_out, flat)


def solution(mesh):
    tiled = P("frame", "band", None, None)
    return jax.shard_map(
        shards, mesh=mesh, in_specs=(tiled, tiled) + (P(),) * 11, out_specs=tiled, check_vma=False
    )
```

```python
import functools
import math

import jax
import jax.numpy as jnp
import numpy as np
from jax import lax
from jax.experimental import pallas as pl
from jax.experimental.pallas import tpu as pltpu
from jax.sharding import PartitionSpec as P

BF = jnp.bfloat16
F32 = jnp.float32
GROUP = 4
VMEM_BYTES = 36 * 1024 * 1024


def tapped(dst, row, tap, value):
    dst[row, :, tap * 256 : tap * 256 + 256] = value[:, :256]
    dst[row, :, 768 + tap * 64 : 832 + tap * 64] = value[:, 256:]


def arrange(dst, weight):
    for dy in range(3):
        for dx in range(3):
            w = weight[dy, dx]
            top = slice(dy * 256, dy * 256 + 256)
            low = slice(768 + dy * 64, 832 + dy * 64)
            left = slice(dx * 256, dx * 256 + 256)
            right = slice(768 + dx * 64, 832 + dx * 64)
            dst[top, left] = w[:256, :256]
            dst[top, right] = w[:256, 256:]
            dst[low, left] = w[256:, :256]
            dst[low, right] = w[256:, 256:]


def combine(prod, rows):
    def shifted(a, b, c):
        gap = jnp.zeros((8, a.shape[1]), F32)
        return (
            b
            + jnp.concatenate([gap, a[:-8]], axis=0)
            + jnp.concatenate([c[8:], gap], axis=0)
        )

    main = shifted(prod[rows, 0:256], prod[rows, 256:512], prod[rows, 512:768])
    rest = shifted(prod[rows, 768:832], prod[rows, 832:896], prod[rows, 896:960])
    return jnp.concatenate([main, rest], axis=1)


def conv_kernel(
    meta, frames, control, low, high, first, second, table, gain,
    out0, out1, out2, out3, flat,
    merged, taps1, taps2, wide1, wide2, prod, normed,
):
    me = meta[0]

    def put(row, f, value):
        value = value.astype(BF).astype(F32)
        rest = jnp.concatenate([value[:, 256:], jnp.zeros((16, 64), F32)], axis=1)
        for j, part in enumerate((value[:, :128], value[:, 128:256], rest)):
            merged[j, row, pl.ds(f, 16, stride=8), :] = part

    def taken(row):
        return jnp.concatenate([merged[0, row], merged[1, row], merged[2, row, :, :64]], axis=1)

    for f in range(8):
        for y in range(8):
            put(y + 2, f, frames[f, y].astype(F32) + control[f, y].astype(F32))
        for y in range(2):
            put(y, f, low[f, y].astype(F32))
            put(y + 10, f, high[f, y].astype(F32))
    for m in range(12):
        value = taken(m).astype(BF)
        for dy in range(3):
            if 0 <= m - dy < 10:
                tapped(taps1, m - dy, dy, value)
    arrange(wide1, first)
    arrange(wide2, second)
    embed = table[...]
    for part in range(2):
        prod[...] = jnp.dot(
            taps1[part * 5 : part * 5 + 5].reshape(640, 960), wide1[...],
            preferred_element_type=F32,
        )
        for i in range(5):
            row = part * 5 + i
            t = combine(prod, slice(i * 128, i * 128 + 128)) + embed
            act = t * (0.5 * jnp.tanh(0.5 * t) + 0.5)
            if row == 0:
                act = jnp.where(meta[1] == 1, 0.0, act)
            if row == 9:
                act = jnp.where(meta[2] == 1, 0.0, act)
            act = act.astype(BF)
            for dy in range(3):
                if 0 <= row - dy < 8:
                    tapped(taps2, row - dy, dy, act)
    for part in range(2):
        prod[0:512, :] = jnp.dot(
            taps2[part * 4 : part * 4 + 4].reshape(512, 960), wide2[...],
            preferred_element_type=F32,
        )
        for i in range(4):
            y = part * 4 + i
            block = combine(prod, slice(i * 128, i * 128 + 128)) + taken(y + 2)
            flat[y] = block
            mean = jnp.sum(block, axis=1, keepdims=True) * (1.0 / 320)
            centre = block - mean
            var = jnp.sum(centre * centre, axis=1, keepdims=True) * (1.0 / 320)
            normed[y] = (centre * lax.rsqrt(var + 1e-5) * gain[...]).astype(BF)
    for k, out in enumerate((out0, out1, out2, out3)):
        out[...] = normed[pl.ds(2 * (me ^ k), 2)].reshape(256, 320)


def attend_kernel(
    meta, own0, own1, own2, own3, halo0, halo1, halo2, halo3, wq, wk, wv, bias,
    out0, out1, out2, out3,
    field, query, key, value, score, prob, back,
):
    me = meta[0]
    pixels = field.shape[0]
    for k, own in enumerate((own0, own1, own2, own3)):
        at = pl.multiple_of(16 + 8 * (me ^ k), 8)
        field[:, pl.ds(at, 8), :] = own[...].astype(F32).reshape(pixels, 8, 320)
    for k, halo in enumerate((halo0, halo1, halo2, halo3)):
        block = me ^ k
        at = pl.multiple_of(jnp.where(block >= 2, 8 * block - 16, 48 + 8 * block), 8)
        field[:, pl.ds(at, 8), :] = halo[...].astype(F32).reshape(pixels, 8, 320)

    def project(x, w):
        return jnp.dot(x, w[...], preferred_element_type=F32).astype(BF)

    x = field[...].reshape(pixels * 64, 320).astype(BF)
    key[...] = project(x, wk).reshape(pixels, 64, 320)
    value[...] = project(x, wv).reshape(pixels, 64, 320)
    x = field[:, 16:48, :].reshape(pixels * 32, 320).astype(BF)
    query[...] = project(x, wq).reshape(pixels, 32, 320)

    def heads_at(lanes, base):
        lane = lax.broadcasted_iota(jnp.int32, (4, 1, lanes), 2)
        first = base + 40 * lax.broadcasted_iota(jnp.int32, (4, 1, lanes), 0)
        return ((lane >= first) & (lane < first + 40)).astype(F32).astype(BF)

    spread_low = heads_at(256, 0)
    spread_high = heads_at(192, 32)
    scale = 40.0**-0.5 / math.log(2.0)
    across = (((1,), (1,)), ((), ()))

    def scores(p):
        q = query[p]
        k = key[p]
        low = (q[None, :, 0:256] * spread_low).reshape(128, 256)
        high = (q[None, :, 128:320] * spread_high).reshape(128, 192)
        score[p, :, 0:128] = lax.dot_general(
            k[:, 0:256], low, across, preferred_element_type=F32
        )
        score[p, :, 128:256] = lax.dot_general(
            k[:, 128:320], high, across, preferred_element_type=F32
        )

    def softmax(p):
        s = score[p] * scale + bias[...]
        e = jnp.exp2(s - jnp.max(s, axis=0, keepdims=True))
        prob[p] = (e * (1.0 / jnp.sum(e, axis=0, keepdims=True))).astype(BF)

    def inside(h, lanes, base):
        lane = lax.broadcasted_iota(jnp.int32, (1, lanes), 1) + base
        return (lane >= 40 * h) & (lane < 40 * h + 40)

    def attended(p):
        w = prob[p].T
        v = value[p]
        low = jnp.dot(w[0:128], v[:, 0:256], preferred_element_type=F32)
        high = jnp.dot(w[128:256], v[:, 128:320], preferred_element_type=F32)
        left = low[0:32, 0:128]
        for h in (1, 2, 3):
            left = jnp.where(inside(h, 128, 0), low[32 * h : 32 * h + 32, 0:128], left)
        middle = low[96:128, 128:256]
        for h in (4, 5, 6):
            at = 32 * h - 128
            middle = jnp.where(inside(h, 128, 128), high[at : at + 32, 0:128], middle)
        right = jnp.where(inside(7, 64, 256), high[96:128, 128:192], high[64:96, 128:192])
        att = jnp.concatenate([left, middle, right], axis=1)
        for b in range(4):
            back[b, p] = att[8 * b : 8 * b + 8]

    def each(step):
        def some(i, carry):
            for j in range(16):
                step(i * 16 + j)
            return carry

        lax.fori_loop(0, pixels // 16, some, 0)

    each(scores)
    each(softmax)
    each(attended)
    for k, out in enumerate((out0, out1, out2, out3)):
        out[...] = back[me ^ k].reshape(pixels * 8, 320).astype(BF)


def final_kernel(meta, a0, a1, a2, a3, w_out, flat, out, total):
    k = pl.program_id(0)
    for at, a in enumerate((a0, a1, a2, a3)):

        @pl.when(k == at)
        def _():
            mixed = jnp.dot(a[...], w_out[...], preferred_element_type=F32)
            mixed = flat[...].reshape(256, 320) + mixed
            total[0] = mixed[:, :128]
            total[1] = mixed[:, 128:256]
            total[2, :, :64] = mixed[:, 256:]

    for f in range(8):
        for y in range(2):
            for j, width in enumerate((128, 128, 64)):
                part = total[j, pl.ds(y * 128 + f, 16, stride=8), :]
                out[f, y, :, j * 128 : j * 128 + width] = part[:, :width]


def shards(
    frames, control, conv_first, conv_second, time_table, step_index, norm_gain,
    w_query, w_key, w_value, w_out, rel_bias, reach,
):
    count = lax.axis_size("frame")
    bands = lax.axis_size("band")
    planes = count // GROUP
    place = lax.axis_index("frame")
    band = lax.axis_index("band")
    me = place % GROUP
    meta = jnp.stack(
        [me, (band == 0).astype(jnp.int32), (band == bands - 1).astype(jnp.int32)]
    ).astype(jnp.int32)

    up = [(i, i + 1) for i in range(bands - 1)]
    down = [(i + 1, i) for i in range(bands - 1)]

    def edge(rows):
        return (frames[:, rows].astype(F32) + control[:, rows].astype(F32)).astype(BF)

    low = lax.ppermute(edge(slice(6, 8)), "band", up)
    high = lax.ppermute(edge(slice(0, 2)), "band", down)

    delta = np.arange(64)[None, :] - 16 - np.arange(32)[:, None]
    picks = (delta[:, :, None] + 16 == np.arange(33)[None, None, :]).astype(np.float32)
    bias = jnp.einsum("hs,ijs->hij", rel_bias, picks, precision=lax.Precision.HIGHEST)
    reach_q = lax.dynamic_slice_in_dim(reach, (place // GROUP) * 32, 32)
    allowed = np.abs(delta) <= reach_q[:, None]
    bias = jnp.where(allowed[None], bias * (1.0 / math.log(2.0)), -jnp.inf).reshape(256, 64).T

    whole = pl.BlockSpec(memory_space=pltpu.VMEM)
    smem = pl.BlockSpec(memory_space=pltpu.SMEM)
    params = pltpu.CompilerParams(vmem_limit_bytes=VMEM_BYTES)
    piece = jax.ShapeDtypeStruct((256, 320), BF)

    def at(shape):
        return pl.BlockSpec(shape, lambda i, m: (0,) * len(shape))

    embed = lax.dynamic_slice_in_dim(time_table, step_index[0], 1)
    n0, n1, n2, n3, flat = pl.pallas_call(
        conv_kernel,
        in_specs=[smem] + [whole] * 8,
        out_specs=[whole] * 5,
        scratch_shapes=[
            pltpu.VMEM((3, 12, 128, 128), F32),
            pltpu.VMEM((10, 128, 960), BF),
            pltpu.VMEM((8, 128, 960), BF),
            pltpu.VMEM((960, 960), BF),
            pltpu.VMEM((960, 960), BF),
            pltpu.VMEM((640, 960), F32),
            pltpu.VMEM((8, 128, 320), BF),
        ],
        out_shape=[piece] * 4 + [jax.ShapeDtypeStruct((8, 128, 320), F32)],
        compiler_params=params,
        name="conv_block",
    )(meta, frames, control, low, high, conv_first, conv_second, embed, norm_gain[None])

    pieces = (n0, n1, n2, n3)

    def plane(i, k):
        return (i & ~3) | ((i & 3) ^ k)

    def exchange(x, k):
        return lax.ppermute(x, "frame", [(i, plane(i, k)) for i in range(count)])

    def beside(i, k):
        turn = 1 if i & 2 else -1
        return (((i >> 2) + turn) % planes) * GROUP + ((i & 3) ^ k)

    own = [n0] + [exchange(pieces[k], k) for k in (1, 2, 3)]
    halo = [
        lax.ppermute(pieces[k], "frame", [(i, beside(i, k)) for i in range(count)])
        for k in (0, 1)
    ]
    for k in (2, 3):
        route = [
            (i, (((i >> 2) + (1 if (i ^ k) & 2 else -1)) % planes) * GROUP + (i & 3))
            for i in range(count)
        ]
        halo.append(lax.ppermute(own[k], "frame", route))

    outs = pl.pallas_call(
        attend_kernel,
        in_specs=[smem] + [whole] * 12,
        out_specs=[whole] * 4,
        out_shape=[piece] * 4,
        scratch_shapes=[
            pltpu.VMEM((32, 64, 320), F32),
            pltpu.VMEM((32, 32, 320), BF),
            pltpu.VMEM((32, 64, 320), BF),
            pltpu.VMEM((32, 64, 320), BF),
            pltpu.VMEM((32, 64, 256), F32),
            pltpu.VMEM((32, 64, 256), BF),
            pltpu.VMEM((4, 32, 8, 320), F32),
        ],
        compiler_params=params,
        name="attend",
    )(meta, *own, *halo, w_query, w_key, w_value, bias)

    back = [outs[0]] + [exchange(outs[k], k) for k in (1, 2, 3)]

    return pl.pallas_call(
        final_kernel,
        grid_spec=pltpu.PrefetchScalarGridSpec(
            num_scalar_prefetch=1,
            grid=(4,),
            in_specs=[at((256, 320))] * 4
            + [at((320, 320)), pl.BlockSpec((2, 128, 320), lambda i, m: (m[0] ^ i, 0, 0))],
            out_specs=pl.BlockSpec((8, 2, 16, 320), lambda i, m: (0, m[0] ^ i, 0, 0)),
            scratch_shapes=[pltpu.VMEM((3, 256, 128), F32)],
        ),
        out_shape=jax.ShapeDtypeStruct((8, 8, 16, 320), F32),
        compiler_params=params,
        name="project_out",
    )(meta, *back, w_out, flat)


def solution(mesh):
    tiled = P("frame", "band", None, None)
    return jax.shard_map(
        shards, mesh=mesh, in_specs=(tiled, tiled) + (P(),) * 11, out_specs=tiled, check_vma=False
    )
```

```python
import math

import jax
import jax.numpy as jnp
from jax import lax
from jax.experimental import pallas as pl
from jax.experimental.pallas import tpu as pltpu
from jax.sharding import PartitionSpec as P

BF = jnp.bfloat16
F32 = jnp.float32
GROUP = 4
MIB = 1024 * 1024


def tapped(dst, row, tap, value):
    dst[row, :, tap * 256 : tap * 256 + 256] = value[:, :256]
    dst[row, :, 768 + tap * 64 : 832 + tap * 64] = value[:, 256:]


def arrange(dst, weight):
    for dy in range(3):
        for dx in range(3):
            w = weight[dy, dx]
            top = slice(dy * 256, dy * 256 + 256)
            low = slice(768 + dy * 64, 832 + dy * 64)
            left = slice(dx * 256, dx * 256 + 256)
            right = slice(768 + dx * 64, 832 + dx * 64)
            dst[top, left] = w[:256, :256]
            dst[top, right] = w[:256, 256:]
            dst[low, left] = w[256:, :256]
            dst[low, right] = w[256:, 256:]


def combine(prod, row):
    rows = slice(row * 128, row * 128 + 128)

    def shifted(a, b, c):
        gap = jnp.zeros((8, a.shape[1]), F32)
        return (
            b
            + jnp.concatenate([gap, a[:-8]], axis=0)
            + jnp.concatenate([c[8:], gap], axis=0)
        )

    main = shifted(prod[rows, 0:256], prod[rows, 256:512], prod[rows, 512:768])
    rest = shifted(prod[rows, 768:832], prod[rows, 832:896], prod[rows, 896:960])
    return jnp.concatenate([main, rest], axis=1)


def put(merged, row, f, value):
    value = value.astype(BF).astype(F32)
    rest = jnp.concatenate([value[:, 256:], jnp.zeros((16, 64), F32)], axis=1)
    for j, part in enumerate((value[:, :128], value[:, 128:256], rest)):
        merged[j, row, pl.ds(f, 16, stride=8), :] = part


def taken(merged, row):
    return jnp.concatenate([merged[0, row], merged[1, row], merged[2, row, :, :64]], axis=1)


def multiply(prod, taps, wide, count):
    prod[0 : count * 128, :] = jnp.dot(
        taps[...].reshape(count * 128, 960), wide[...], preferred_element_type=F32
    )


def silu(t):
    return t * (0.5 * jnp.tanh(0.5 * t) + 0.5)


def layer_norm(block, gain):
    mean = jnp.sum(block, axis=1, keepdims=True) * (1.0 / 320)
    centre = block - mean
    var = jnp.sum(centre * centre, axis=1, keepdims=True) * (1.0 / 320)
    return (centre * lax.rsqrt(var + 1e-5) * gain).astype(BF)


def hand_out(me, normed, keep, give):
    keep[0] = normed[me]
    keep[1] = normed[me ^ 2]
    give[0] = normed[me ^ 1]
    give[1] = normed[me ^ 3]


def in_group():
    return lax.axis_index("frame") % GROUP


def edges_kernel(frames, control, top, bottom, fbuf, cbuf, sems):
    loads = []
    for i, (src, dst) in enumerate(((frames, fbuf), (control, cbuf))):
        for j in range(2):
            loads.append(
                pltpu.make_async_copy(src.at[:, pl.ds(6 * j, 2)], dst.at[j], sems.at[2 * j + i])
            )
    for load in loads:
        load.start()
    for j, out in ((1, bottom), (0, top)):
        loads[j].wait()
        loads[2 + j].wait()
        out[...] = (fbuf[j].astype(F32) + cbuf[j].astype(F32)).astype(BF)


def inner_kernel(
    step, frames, control, first, second, table, gain,
    keep, give, flat, edge, rim, wide1, wide2, vectors,
    column, tail, row, fbuf, cbuf, buf1, buf2, merged, taps1, taps2, prod, normed, sems,
):
    loads = [
        pltpu.make_async_copy(src, dst, sems.at[i])
        for i, (src, dst) in enumerate(
            ((frames, fbuf), (control, cbuf), (first, buf1), (second, buf2))
        )
    ]
    for load in loads[:3]:
        load.start()
    me = in_group()
    block = step[0] // 128
    whole_block = pltpu.make_async_copy(
        table.at[:, pl.ds(pl.multiple_of(jnp.minimum(block, 6) * 128, 128), 128)],
        column, sems.at[4],
    )
    last_block = pltpu.make_async_copy(
        table.at[:, pl.ds(896, 104)], tail, sems.at[4]
    )

    @pl.when(block < 7)
    def _():
        whole_block.start()
        whole_block.wait()
        row[...] = column[...].T

    @pl.when(block >= 7)
    def _():
        last_block.start()
        last_block.wait()
        row[0:104] = tail[...].T

    embed = row[pl.ds(step[0] % 128, 1), :]
    vectors[0:1] = embed
    vectors[1:2] = gain[...].reshape(1, 320)
    gain = vectors[1:2]
    loads[0].wait()
    loads[1].wait()
    loads[3].start()
    for m in range(8):
        for f in range(8):
            put(merged, m, f, fbuf[f, m].astype(F32) + cbuf[f, m].astype(F32))
        value = taken(merged, m).astype(BF)
        if m in (0, 1, 6, 7):
            rim[(0, 1, None, None, None, None, 2, 3)[m]] = value
        for dy in range(3):
            if 0 <= m - dy < 6:
                tapped(taps1, m - dy, dy, value)
    loads[2].wait()
    arrange(wide1, buf1)
    multiply(prod, taps1, wide1, 6)
    for r in range(6):
        act = silu(combine(prod, r) + embed).astype(BF)
        for dy in range(3):
            if 0 <= r - dy < 4:
                tapped(taps2, r - dy, dy, act)
        if r in (0, 1, 4, 5):
            edge[(0, 1, None, None, 2, 3)[r]] = act
    loads[3].wait()
    arrange(wide2, buf2)
    multiply(prod, taps2, wide2, 4)
    for y in range(4):
        value = combine(prod, y) + taken(merged, y + 2)
        flat[y] = value
        normed[y] = layer_norm(value, gain)
    hand_out(me, normed, keep, give)


def outer_kernel(
    low, high, rim, edge, wide1, wide2, vectors,
    keep, give, flat,
    merged, taps1, taps2, prod, normed,
):
    me = in_group()
    band = lax.axis_index("band")
    embed = vectors[0:1]
    gain = vectors[1:2]
    for f in range(8):
        for y in range(2):
            put(merged, y, f, low[f, y].astype(F32))
            put(merged, 2 + y, f, high[f, y].astype(F32))
    rows = [taken(merged, i).astype(BF) for i in range(4)]
    rows = [rows[0], rows[1], rim[0], rim[1], rim[2], rim[3], rows[2], rows[3]]
    starts = (0, 1, 4, 5)
    for m in range(8):
        for r in range(4):
            if 0 <= m - starts[r] < 3:
                tapped(taps1, r, m - starts[r], rows[m])
    multiply(prod, taps1, wide1, 4)
    act = [silu(combine(prod, r) + embed) for r in range(4)]
    act[0] = jnp.where(band == 0, 0.0, act[0])
    act[3] = jnp.where(band == lax.axis_size("band") - 1, 0.0, act[3])
    act = [a.astype(BF) for a in act]
    lines = ((act[0], act[1], edge[0], edge[1]), (edge[2], edge[3], act[2], act[3]))
    for side in range(2):
        for i in range(4):
            for dy in range(3):
                if 0 <= i - dy < 2:
                    tapped(taps2, 2 * side + i - dy, dy, lines[side][i])
    multiply(prod, taps2, wide2, 4)
    for y in range(4):
        value = combine(prod, y) + rim[y].astype(F32)
        flat[y] = value
        normed[y] = layer_norm(value, gain)
    hand_out(me, normed, keep, give)


def pack_kernel(keep, got, near, far):
    near[0] = keep[0]
    near[1] = got[0]
    far[0] = keep[1]
    far[1] = got[1]


def attend_kernel(
    reach, near, across_x, near_z, across_z, wq, wk, wv, w_out, rel_bias,
    out0, out1, out2, out3,
    weights, field, query, key, value, score, prob, back, bias, sems,
):
    loads = [
        pltpu.make_async_copy(w, weights.at[i], sems.at[i])
        for i, w in enumerate((wq, wk, wv, w_out))
    ]
    for load in loads:
        load.start()
    place = lax.axis_index("frame")
    me = place % GROUP
    pixels = field.shape[0]

    line = lax.broadcasted_iota(jnp.int32, (64, 128), 0)
    lane = lax.broadcasted_iota(jnp.int32, (64, 128), 1) % 32
    limit = jnp.zeros((1, 128), jnp.int32)
    for i in range(32):
        limit = jnp.where(lane[0:1] == i, reach[(place // GROUP) * 32 + i], limit)
    allowed = jnp.abs(line - 16 - lane) <= limit
    padded = jnp.concatenate([rel_bias[...], jnp.zeros((8, 95), F32)], axis=1)
    for half in range(2):
        table = []
        for h in range(4 * half, 4 * half + 4):
            wide = jnp.broadcast_to(padded[h : h + 1], (32, 128))
            table.append(pltpu.roll(wide, 0, 1, stride=1, stride_axis=0))
        table = jnp.concatenate(table, axis=0).T[0:64]
        bias[:, half * 128 : half * 128 + 128] = jnp.where(
            allowed, table * (1.0 / math.log(2.0)), -jnp.inf
        )

    for k in range(4):
        block = me ^ k
        own = (near, across_x)[k // 2]
        at = pl.multiple_of(16 + 8 * block, 8)
        field[:, pl.ds(at, 8), :] = own[k % 2].astype(F32).reshape(pixels, 8, 320)
        halo = (near_z, across_z)[k // 2]
        at = pl.multiple_of(jnp.where(block >= 2, 8 * block - 16, 48 + 8 * block), 8)
        field[:, pl.ds(at, 8), :] = halo[k % 2].astype(F32).reshape(pixels, 8, 320)
    for load in loads[:3]:
        load.wait()

    def project(x, i):
        return jnp.dot(x, weights[i], preferred_element_type=F32).astype(BF)

    x = field[...].reshape(pixels * 64, 320).astype(BF)
    key[...] = project(x, 1).reshape(pixels, 64, 320)
    value[...] = project(x, 2).reshape(pixels, 64, 320)
    x = field[:, 16:48, :].reshape(pixels * 32, 320).astype(BF)
    query[...] = project(x, 0).reshape(pixels, 32, 320)

    def heads_at(lanes, base):
        lane = lax.broadcasted_iota(jnp.int32, (4, 1, lanes), 2)
        first = base + 40 * lax.broadcasted_iota(jnp.int32, (4, 1, lanes), 0)
        return ((lane >= first) & (lane < first + 40)).astype(F32).astype(BF)

    spread_low = heads_at(256, 0)
    spread_high = heads_at(192, 32)
    scale = 40.0**-0.5 / math.log(2.0)
    across = (((1,), (1,)), ((), ()))

    def scores(p):
        q = query[p]
        k = key[p]
        low = (q[None, :, 0:256] * spread_low).reshape(128, 256)
        high = (q[None, :, 128:320] * spread_high).reshape(128, 192)
        score[p, :, 0:128] = lax.dot_general(
            k[:, 0:256], low, across, preferred_element_type=F32
        )
        score[p, :, 128:256] = lax.dot_general(
            k[:, 128:320], high, across, preferred_element_type=F32
        )

    def softmax(p):
        s = score[p] * scale + bias[...]
        e = jnp.exp2(s - jnp.max(s, axis=0, keepdims=True))
        prob[p] = (e * (1.0 / jnp.sum(e, axis=0, keepdims=True))).astype(BF)

    def inside(h, lanes, base):
        lane = lax.broadcasted_iota(jnp.int32, (1, lanes), 1) + base
        return (lane >= 40 * h) & (lane < 40 * h + 40)

    def attended(p):
        w = prob[p].T
        v = value[p]
        low = jnp.dot(w[0:128], v[:, 0:256], preferred_element_type=F32)
        high = jnp.dot(w[128:256], v[:, 128:320], preferred_element_type=F32)
        left = low[0:32, 0:128]
        for h in (1, 2, 3):
            left = jnp.where(inside(h, 128, 0), low[32 * h : 32 * h + 32, 0:128], left)
        middle = low[96:128, 128:256]
        for h in (4, 5, 6):
            at = 32 * h - 128
            middle = jnp.where(inside(h, 128, 128), high[at : at + 32, 0:128], middle)
        right = jnp.where(inside(7, 64, 256), high[96:128, 128:192], high[64:96, 128:192])
        att = jnp.concatenate([left, middle, right], axis=1)
        for b in range(4):
            back[b, p] = att[8 * b : 8 * b + 8]

    def each(step):
        def some(i, carry):
            for j in range(16):
                step(i * 16 + j)
            return carry

        lax.fori_loop(0, pixels // 16, some, 0)

    each(scores)
    each(softmax)
    each(attended)
    loads[3].wait()
    for k, out in enumerate((out0, out1, out2, out3)):
        out[...] = project(back[me ^ k].reshape(pixels * 8, 320).astype(BF), 3)


def final_kernel(first_row, second_row, *refs):
    a0, a1, a2, a3, flat = refs[:5]
    me = in_group()
    out, total, done, sems = refs[-4:]
    stores = []
    for k, a in enumerate((a0, a1, a2, a3)):
        q = me ^ k
        row = jnp.where(q >= 2, second_row + q - 2, first_row + q)
        value = a[...].astype(F32) + flat[q]
        rest = jnp.concatenate([value[:, 256:], jnp.zeros((128, 64), F32)], axis=1)
        for j, part in enumerate((value[:, :128], value[:, 128:256], rest)):
            total[k, j] = part
        for f in range(8):
            for j, width in enumerate((128, 128, 64)):
                part = total[k, j, pl.ds(f, 16, stride=8), :]
                done[k, f, :, j * 128 : j * 128 + width] = part[:, :width]
        store = pltpu.make_async_copy(done.at[k], out.at[:, row], sems.at[k])
        store.start()
        stores.append(store)
    for store in stores:
        store.wait()


def shards(
    frames, control, conv_first, conv_second, time_table, step_index, norm_gain,
    w_query, w_key, w_value, w_out, rel_bias, reach,
):
    count = lax.axis_size("frame")
    bands = lax.axis_size("band")
    planes = count // GROUP
    up = [(i, i + 1) for i in range(bands - 1)]
    down = [(i + 1, i) for i in range(bands - 1)]

    def plane(i, k):
        return (i & ~3) | ((i & 3) ^ k)

    def beside(i, k):
        turn = 1 if i & 2 else -1
        return (((i >> 2) + turn) % planes) * GROUP + ((i & 3) ^ k)

    def exchange(x, to, k):
        return lax.ppermute(x, "frame", [(i, to(i, k)) for i in range(count)])

    vmem = pl.BlockSpec(memory_space=pltpu.VMEM)
    smem = pl.BlockSpec(memory_space=pltpu.SMEM)
    anywhere = pl.BlockSpec(memory_space=pltpu.HBM)

    def params(mebibytes):
        return pltpu.CompilerParams(vmem_limit_bytes=mebibytes * MIB)
    pair = jax.ShapeDtypeStruct((2, 128, 320), BF)
    chunk = pltpu.VMEM((4, 128, 320), F32)
    wide = pltpu.VMEM((960, 960), BF)
    rows = pltpu.VMEM((4, 128, 320), BF)

    def cost(flops):
        return pl.CostEstimate(flops=flops, bytes_accessed=4_000_000, transcendentals=0)

    def stay(*arrays):
        return [pltpu.with_memory_space_constraint(x, pltpu.HBM) for x in arrays]

    def near_by(*arrays):
        return [pltpu.with_memory_space_constraint(x, pltpu.VMEM) for x in arrays]

    rows_scratch = [
        pltpu.VMEM((4, 128, 960), BF),
        pltpu.VMEM((768, 960), F32),
        pltpu.VMEM((4, 128, 320), BF),
    ]
    margin = jax.ShapeDtypeStruct((8, 2, 16, 320), BF)
    top, bottom = pl.pallas_call(
        edges_kernel,
        in_specs=[anywhere] * 2,
        out_specs=[vmem] * 2,
        out_shape=[margin] * 2,
        scratch_shapes=[
            pltpu.VMEM((2, 8, 2, 16, 320), BF),
            pltpu.VMEM((2, 8, 2, 16, 320), BF),
            pltpu.SemaphoreType.DMA((4,)),
        ],
        compiler_params=params(4),
        name="edges",
    )(*stay(frames, control))
    top, bottom, step_index = lax.optimization_barrier((top, bottom, step_index))
    low = lax.ppermute(bottom, "band", up)
    high = lax.ppermute(top, "band", down)

    keep, give, flat_in, edge, rim, wide1, wide2, vectors = pl.pallas_call(
        inner_kernel,
        in_specs=[smem] + [anywhere] * 5 + [vmem],
        out_specs=[vmem] * 8,
        out_shape=[pair, pair, chunk, rows, rows, wide, wide, pltpu.VMEM((2, 320), F32)],
        scratch_shapes=[
            pltpu.VMEM((320, 128), F32),
            pltpu.VMEM((320, 104), F32),
            pltpu.VMEM((128, 320), F32),
            pltpu.VMEM((8, 8, 16, 320), BF),
            pltpu.VMEM((8, 8, 16, 320), BF),
            pltpu.VMEM((3, 3, 320, 320), BF),
            pltpu.VMEM((3, 3, 320, 320), BF),
            pltpu.VMEM((3, 8, 128, 128), F32),
            pltpu.VMEM((6, 128, 960), BF),
        ]
        + rows_scratch
        + [pltpu.SemaphoreType.DMA((5,))],
        compiler_params=params(22),
        name="inner_rows",
    )(step_index, *stay(frames, control, conv_first, conv_second, time_table.T), norm_gain)

    keep, give, low, high = lax.optimization_barrier((keep, give, low, high))

    def packed(keep, give):
        got = exchange(give, plane, 1)
        return pl.pallas_call(
            pack_kernel,
            in_specs=[vmem] * 2,
            out_specs=[vmem] * 2,
            out_shape=[pair] * 2,
            compiler_params=params(2),
            name="pack",
        )(keep, got)

    def onward(i, k):
        turn = 1 if (i ^ 2) & 2 else -1
        return (((i >> 2) + turn) % planes) * GROUP + (i & 3)

    near_in, far = packed(keep, give)
    x_in = exchange(far, plane, 2)
    z_in = exchange(near_in, beside, 0)
    near_in, edge = lax.optimization_barrier((near_in, edge))

    keep, give, flat_out = pl.pallas_call(
        outer_kernel,
        in_specs=[vmem] * 7,
        out_specs=[vmem] * 3,
        out_shape=[pair, pair, chunk],
        scratch_shapes=[
            pltpu.VMEM((3, 4, 128, 128), F32),
            pltpu.VMEM((4, 128, 960), BF),
        ]
        + rows_scratch,
        compiler_params=params(12),
        name="outer_rows",
    )(low, high, *near_by(rim, edge, wide1, wide2, vectors))

    give, x_in, z_in = lax.optimization_barrier((give, x_in, z_in))
    xz_in = exchange(x_in, onward, 0)
    near_out, far = packed(keep, give)
    x_out = exchange(far, plane, 2)
    xz_out = exchange(far, beside, 2)
    z_out = exchange(near_out, beside, 0)

    def attend(fields):
        piece = jax.ShapeDtypeStruct((128, 320), BF)
        outs = pl.pallas_call(
            attend_kernel,
            in_specs=[smem] + [vmem] * 4 + [anywhere] * 4 + [vmem],
            out_specs=[vmem] * 4,
            out_shape=[piece] * 4,
            scratch_shapes=[
                pltpu.VMEM((4, 320, 320), BF),
                pltpu.VMEM((16, 64, 320), F32),
                pltpu.VMEM((16, 32, 320), BF),
                pltpu.VMEM((16, 64, 320), BF),
                pltpu.VMEM((16, 64, 320), BF),
                pltpu.VMEM((16, 64, 256), F32),
                pltpu.VMEM((16, 64, 256), BF),
                pltpu.VMEM((4, 16, 8, 320), F32),
                pltpu.VMEM((64, 256), F32),
                pltpu.SemaphoreType.DMA((4,)),
            ],
            compiler_params=params(14),
            name="attend",
        )(reach, *fields, *stay(w_query, w_key, w_value, w_out), rel_bias)
        return [outs[0]] + [exchange(outs[k], plane, k) for k in (2, 3, 1)], outs[0]

    near_out, near_in = lax.optimization_barrier((near_out, near_in))
    (b0, b2, b3, b1), _ = attend((near_in, x_in, z_in, xz_in))
    back_in = [b0, b1, b2, b3]
    (b0, b2, b3, b1), mark = attend((near_out, x_out, z_out, xz_out))
    back_out = [b0, b1, b2, b3]

    def finish(first_row, second_row, back, flat, *before):
        def body(*refs):
            final_kernel(first_row, second_row, *refs)

        return pl.pallas_call(
            body,
            in_specs=[vmem] * 5 + [anywhere] * len(before),
            out_specs=anywhere,
            out_shape=jax.ShapeDtypeStruct(frames.shape, F32),
            input_output_aliases={5: 0} if before else {},
            scratch_shapes=[
                pltpu.VMEM((4, 3, 128, 128), F32),
                pltpu.VMEM((4, 8, 16, 320), F32),
                pltpu.SemaphoreType.DMA((4,)),
            ],
            compiler_params=params(6),
            name="project_out",
        )(*back, *near_by(flat), *before)

    back_in[0], mark = lax.optimization_barrier((back_in[0], mark))
    out = finish(2, 4, back_in, flat_in)
    return finish(0, 6, back_out, flat_out, out)


def solution(mesh):
    tiled = P("frame", "band", None, None)
    return jax.shard_map(
        shards, mesh=mesh, in_specs=(tiled, tiled) + (P(),) * 11, out_specs=tiled, check_vma=False
    )
```

```python
import math

import jax
import jax.numpy as jnp
from jax import lax
from jax.experimental import pallas as pl
from jax.experimental.pallas import tpu as pltpu
from jax.sharding import PartitionSpec as P

BF = jnp.bfloat16
F32 = jnp.float32
GROUP = 4
MIB = 1024 * 1024


def tapped(dst, row, tap, value):
    dst[row, :, tap * 256 : tap * 256 + 256] = value[:, :256]
    dst[row, :, 768 + tap * 64 : 832 + tap * 64] = value[:, 256:]


def arrange(dst, weight):
    for dy in range(3):
        for dx in range(3):
            w = weight[dy, dx]
            top = slice(dy * 256, dy * 256 + 256)
            low = slice(768 + dy * 64, 832 + dy * 64)
            left = slice(dx * 256, dx * 256 + 256)
            right = slice(768 + dx * 64, 832 + dx * 64)
            dst[top, left] = w[:256, :256]
            dst[top, right] = w[:256, 256:]
            dst[low, left] = w[256:, :256]
            dst[low, right] = w[256:, 256:]


def combine(prod, row):
    rows = slice(row * 128, row * 128 + 128)

    def shifted(a, b, c):
        gap = jnp.zeros((8, a.shape[1]), F32)
        return (
            b
            + jnp.concatenate([gap, a[:-8]], axis=0)
            + jnp.concatenate([c[8:], gap], axis=0)
        )

    main = shifted(prod[rows, 0:256], prod[rows, 256:512], prod[rows, 512:768])
    rest = shifted(prod[rows, 768:832], prod[rows, 832:896], prod[rows, 896:960])
    return jnp.concatenate([main, rest], axis=1)


def put(merged, row, f, value):
    value = value.astype(BF).astype(F32)
    rest = jnp.concatenate([value[:, 256:], jnp.zeros((16, 64), F32)], axis=1)
    for j, part in enumerate((value[:, :128], value[:, 128:256], rest)):
        merged[j, row, pl.ds(f, 16, stride=8), :] = part


def taken(merged, row):
    return jnp.concatenate([merged[0, row], merged[1, row], merged[2, row, :, :64]], axis=1)


def multiply(prod, taps, wide, count):
    prod[0 : count * 128, :] = jnp.dot(
        taps[...].reshape(count * 128, 960), wide[...], preferred_element_type=F32
    )


def silu(t):
    return t * (0.5 * jnp.tanh(0.5 * t) + 0.5)


def layer_norm(block, gain):
    mean = jnp.sum(block, axis=1, keepdims=True) * (1.0 / 320)
    centre = block - mean
    var = jnp.sum(centre * centre, axis=1, keepdims=True) * (1.0 / 320)
    return (centre * lax.rsqrt(var + 1e-5) * gain).astype(BF)


def bias_table(bias, rel_bias, reach):
    plane = lax.axis_index("frame") // GROUP
    line = lax.broadcasted_iota(jnp.int32, (64, 128), 0)
    lane = lax.broadcasted_iota(jnp.int32, (64, 128), 1) % 32
    limit = jnp.zeros((1, 128), jnp.int32)
    for i in range(32):
        limit = jnp.where(lane[0:1] == i, reach[plane * 32 + i], limit)
    allowed = jnp.abs(line - 16 - lane) <= limit
    padded = jnp.concatenate([rel_bias[...], jnp.zeros((8, 95), F32)], axis=1)
    for half in range(2):
        table = []
        for h in range(4 * half, 4 * half + 4):
            wide = jnp.broadcast_to(padded[h : h + 1], (32, 128))
            table.append(pltpu.roll(wide, 0, 1, stride=1, stride_axis=0))
        table = jnp.concatenate(table, axis=0).T[0:64]
        bias[:, half * 128 : half * 128 + 128] = jnp.where(
            allowed, table * (1.0 / math.log(2.0)), -jnp.inf
        )


def hand_out(me, normed, keep, give):
    keep[0] = normed[me]
    keep[1] = normed[me ^ 2]
    give[0] = normed[me ^ 1]
    give[1] = normed[me ^ 3]


def in_group():
    return lax.axis_index("frame") % GROUP


def odd_band():
    return lax.axis_index("band") % 2 == 1


def merge_kernel(
    frames, control, first, one, two, rows, wide, fbuf, cbuf, buf, merged, sems
):
    loads = [
        pltpu.make_async_copy(src, dst, sems.at[i])
        for i, (src, dst) in enumerate(((frames, fbuf), (control, cbuf), (first, buf)))
    ]
    for load in loads:
        load.start()
    loads[0].wait()
    loads[1].wait()
    for m in range(8):
        for f in range(8):
            put(merged, m, f, fbuf[f, m].astype(F32) + cbuf[f, m].astype(F32))
        rows[m] = taken(merged, m).astype(BF)
    facing = jnp.where(odd_band(), 6, 0)
    one[...] = rows[pl.ds(facing, 2)]
    two[...] = rows[pl.ds(6 - facing, 2)]
    loads[2].wait()
    arrange(wide, buf)


def inner_kernel(
    step, rows, wide1, second, table, gain,
    keep, give, flat, edge, wide2, vectors,
    line, column, tail, row, buf, taps1, taps2, prod, normed, sems,
):
    loads = [pltpu.make_async_copy(second.at[i], buf.at[i], sems.at[i]) for i in range(3)]
    load_gain = pltpu.make_async_copy(gain, line, sems.at[3])
    me = in_group()
    block = step[0] // 128
    whole_block = pltpu.make_async_copy(
        table.at[:, pl.ds(pl.multiple_of(jnp.minimum(block, 6) * 128, 128), 128)],
        column, sems.at[4],
    )
    last_block = pltpu.make_async_copy(
        table.at[:, pl.ds(896, 104)], tail, sems.at[4]
    )

    @pl.when(block < 7)
    def _():
        whole_block.start()

    @pl.when(block >= 7)
    def _():
        last_block.start()

    load_gain.start()
    for load in loads:
        load.start()
    for m in range(8):
        value = rows[m]
        for dy in range(3):
            if 0 <= m - dy < 6:
                tapped(taps1, m - dy, dy, value)
    multiply(prod, taps1, wide1, 6)

    @pl.when(block < 7)
    def _():
        whole_block.wait()
        row[...] = column[...].T

    @pl.when(block >= 7)
    def _():
        last_block.wait()
        row[0:104] = tail[...].T

    embed = row[pl.ds(step[0] % 128, 1), :]
    vectors[0:1] = embed
    load_gain.wait()
    vectors[1:2] = line[...].reshape(1, 320)
    gain = vectors[1:2]
    for r in range(6):
        act = silu(combine(prod, r) + embed).astype(BF)
        for dy in range(3):
            if 0 <= r - dy < 4:
                tapped(taps2, r - dy, dy, act)
        if r in (0, 1, 4, 5):
            edge[(0, 1, None, None, 2, 3)[r]] = act
    for load in loads:
        load.wait()
    arrange(wide2, buf)
    multiply(prod, taps2, wide2, 4)
    for y in range(4):
        value = combine(prod, y) + rows[y + 2].astype(F32)
        flat[y] = value
        normed[y] = layer_norm(value, gain)
    hand_out(me, normed, keep, give)


def outer_kernel(
    reach, one, two, merged, edge, wide1, wide2, vectors, rel_bias, wq, wk, wv, w_out,
    keep, give, flat, weights, bias,
    taps1, taps2, prod, normed, sems,
):
    loads = [
        pltpu.make_async_copy(w, weights.at[i], sems.at[i])
        for i, w in enumerate((wq, wk, wv, w_out))
    ]
    for load in loads:
        load.start()
    me = in_group()
    band = lax.axis_index("band")
    odd = odd_band()
    embed = vectors[0:1]
    gain = vectors[1:2]
    low = [jnp.where(odd, two[y], one[y]) for y in range(2)]
    high = [jnp.where(odd, one[y], two[y]) for y in range(2)]
    rows = low + [merged[0], merged[1], merged[6], merged[7]] + high
    starts = (0, 1, 4, 5)
    for m in range(8):
        for r in range(4):
            if 0 <= m - starts[r] < 3:
                tapped(taps1, r, m - starts[r], rows[m])
    multiply(prod, taps1, wide1, 4)
    act = [silu(combine(prod, r) + embed) for r in range(4)]
    act[0] = jnp.where(band == 0, 0.0, act[0])
    act[3] = jnp.where(band == lax.axis_size("band") - 1, 0.0, act[3])
    act = [a.astype(BF) for a in act]
    lines = ((act[0], act[1], edge[0], edge[1]), (edge[2], edge[3], act[2], act[3]))
    for side in range(2):
        for i in range(4):
            for dy in range(3):
                if 0 <= i - dy < 2:
                    tapped(taps2, 2 * side + i - dy, dy, lines[side][i])
    multiply(prod, taps2, wide2, 4)
    for y in range(4):
        value = combine(prod, y) + merged[(0, 1, 6, 7)[y]].astype(F32)
        flat[y] = value
        normed[y] = layer_norm(value, gain)
    hand_out(me, normed, keep, give)
    bias_table(bias, rel_bias, reach)
    for load in loads:
        load.wait()


def pack_kernel(keep, got, near, far):
    near[0] = keep[0]
    near[1] = got[0]
    far[0] = keep[1]
    far[1] = got[1]


def attend_kernel(
    near, across_x, near_z, across_z, weights, bias,
    out0, out1, out2, out3,
    field, query, key, value, score, prob, back,
):
    me = in_group()
    pixels = field.shape[0]

    for k in range(4):
        block = me ^ k
        own = (near, across_x)[k // 2]
        at = pl.multiple_of(16 + 8 * block, 8)
        field[:, pl.ds(at, 8), :] = own[k % 2].astype(F32).reshape(pixels, 8, 320)
        halo = (near_z, across_z)[k // 2]
        at = pl.multiple_of(jnp.where(block >= 2, 8 * block - 16, 48 + 8 * block), 8)
        field[:, pl.ds(at, 8), :] = halo[k % 2].astype(F32).reshape(pixels, 8, 320)

    def project(x, i):
        return jnp.dot(x, weights[i], preferred_element_type=F32).astype(BF)

    x = field[...].reshape(pixels * 64, 320).astype(BF)
    key[...] = project(x, 1).reshape(pixels, 64, 320)
    value[...] = project(x, 2).reshape(pixels, 64, 320)
    x = field[:, 16:48, :].reshape(pixels * 32, 320).astype(BF)
    query[...] = project(x, 0).reshape(pixels, 32, 320)

    def heads_at(lanes, base):
        lane = lax.broadcasted_iota(jnp.int32, (4, 1, lanes), 2)
        first = base + 40 * lax.broadcasted_iota(jnp.int32, (4, 1, lanes), 0)
        return ((lane >= first) & (lane < first + 40)).astype(F32).astype(BF)

    spread_low = heads_at(256, 0)
    spread_high = heads_at(192, 32)
    scale = 40.0**-0.5 / math.log(2.0)
    across = (((1,), (1,)), ((), ()))

    def scores(p):
        q = query[p]
        k = key[p]
        low = (q[None, :, 0:256] * spread_low).reshape(128, 256)
        high = (q[None, :, 128:320] * spread_high).reshape(128, 192)
        score[p, :, 0:128] = lax.dot_general(
            k[:, 0:256], low, across, preferred_element_type=F32
        )
        score[p, :, 128:256] = lax.dot_general(
            k[:, 128:320], high, across, preferred_element_type=F32
        )

    def softmax(p):
        s = score[p] * scale + bias[...]
        e = jnp.exp2(s - jnp.max(s, axis=0, keepdims=True))
        prob[p] = (e * (1.0 / jnp.sum(e, axis=0, keepdims=True))).astype(BF)

    def inside(h, lanes, base):
        lane = lax.broadcasted_iota(jnp.int32, (1, lanes), 1) + base
        return (lane >= 40 * h) & (lane < 40 * h + 40)

    def attended(p):
        w = prob[p].T
        v = value[p]
        low = jnp.dot(w[0:128], v[:, 0:256], preferred_element_type=F32)
        high = jnp.dot(w[128:256], v[:, 128:320], preferred_element_type=F32)
        left = low[0:32, 0:128]
        for h in (1, 2, 3):
            left = jnp.where(inside(h, 128, 0), low[32 * h : 32 * h + 32, 0:128], left)
        middle = low[96:128, 128:256]
        for h in (4, 5, 6):
            at = 32 * h - 128
            middle = jnp.where(inside(h, 128, 128), high[at : at + 32, 0:128], middle)
        right = jnp.where(inside(7, 64, 256), high[96:128, 128:192], high[64:96, 128:192])
        att = jnp.concatenate([left, middle, right], axis=1)
        for b in range(4):
            back[b, p] = att[8 * b : 8 * b + 8]

    def each(step):
        def some(i, carry):
            for j in range(16):
                step(i * 16 + j)
            return carry

        lax.fori_loop(0, pixels // 16, some, 0)

    each(scores)
    each(softmax)
    each(attended)
    for k, out in enumerate((out0, out1, out2, out3)):
        out[...] = project(back[me ^ k].reshape(pixels * 8, 320).astype(BF), 3)


def final_kernel(first_row, second_row, *refs):
    a0, a1, a2, a3, flat = refs[:5]
    me = in_group()
    out, total, done, sems = refs[-4:]
    stores = []
    for k, a in enumerate((a0, a1, a2, a3)):
        q = me ^ k
        row = jnp.where(q >= 2, second_row + q - 2, first_row + q)
        value = a[...].astype(F32) + flat[q]
        rest = jnp.concatenate([value[:, 256:], jnp.zeros((128, 64), F32)], axis=1)
        for j, part in enumerate((value[:, :128], value[:, 128:256], rest)):
            total[k, j] = part
        for f in range(8):
            for j, width in enumerate((128, 128, 64)):
                part = total[k, j, pl.ds(f, 16, stride=8), :]
                done[k, f, :, j * 128 : j * 128 + width] = part[:, :width]
        store = pltpu.make_async_copy(done.at[k], out.at[:, row], sems.at[k])
        store.start()
        stores.append(store)
    for store in stores:
        store.wait()


def shards(
    frames, control, conv_first, conv_second, time_table, step_index, norm_gain,
    w_query, w_key, w_value, w_out, rel_bias, reach,
):
    count = lax.axis_size("frame")
    bands = lax.axis_size("band")
    planes = count // GROUP
    def swaps(first):
        pairs = [(i, i + 1) for i in range(first, bands - 1, 2)]
        return pairs + [(j, i) for i, j in pairs]

    def plane(i, k):
        return (i & ~3) | ((i & 3) ^ k)

    def beside(i, k):
        turn = 1 if i & 2 else -1
        return (((i >> 2) + turn) % planes) * GROUP + ((i & 3) ^ k)

    def exchange(x, to, k):
        return lax.ppermute(x, "frame", [(i, to(i, k)) for i in range(count)])

    vmem = pl.BlockSpec(memory_space=pltpu.VMEM)
    smem = pl.BlockSpec(memory_space=pltpu.SMEM)
    anywhere = pl.BlockSpec(memory_space=pltpu.HBM)

    def params(mebibytes):
        return pltpu.CompilerParams(vmem_limit_bytes=mebibytes * MIB)
    pair = jax.ShapeDtypeStruct((2, 128, 320), BF)
    chunk = pltpu.VMEM((4, 128, 320), F32)

    def cost(flops):
        return pl.CostEstimate(flops=flops, bytes_accessed=4_000_000, transcendentals=0)

    def stay(*arrays):
        return [pltpu.with_memory_space_constraint(x, pltpu.HBM) for x in arrays]

    def near_by(*arrays):
        return [pltpu.with_memory_space_constraint(x, pltpu.VMEM) for x in arrays]

    rows_scratch = [
        pltpu.VMEM((4, 128, 960), BF),
        pltpu.VMEM((768, 960), F32),
        pltpu.VMEM((4, 128, 320), BF),
    ]
    wide = pltpu.VMEM((960, 960), BF)
    one, two, merged, wide1 = pl.pallas_call(
        merge_kernel,
        in_specs=[anywhere] * 3,
        out_specs=[vmem] * 4,
        out_shape=[pair, pair, pltpu.VMEM((8, 128, 320), BF), wide],
        scratch_shapes=[
            pltpu.VMEM((8, 8, 16, 320), BF),
            pltpu.VMEM((8, 8, 16, 320), BF),
            pltpu.VMEM((3, 3, 320, 320), BF),
            pltpu.VMEM((3, 8, 128, 128), F32),
            pltpu.SemaphoreType.DMA((3,)),
        ],
        compiler_params=params(8),
        name="merge",
    )(*stay(frames, control, conv_first))
    one, two, step_index = lax.optimization_barrier((one, two, step_index))
    one = lax.ppermute(one, "band", swaps(1))
    two = lax.ppermute(two, "band", swaps(0))

    keep, give, flat_in, edge, wide2, vectors = pl.pallas_call(
        inner_kernel,
        in_specs=[smem] + [vmem] * 2 + [anywhere] * 3,
        out_specs=[vmem] * 6,
        out_shape=[
            pair, pair, chunk, pltpu.VMEM((4, 128, 320), BF), wide, pltpu.VMEM((2, 320), F32)
        ],
        scratch_shapes=[
            pltpu.VMEM((320,), F32),
            pltpu.VMEM((320, 128), F32),
            pltpu.VMEM((320, 104), F32),
            pltpu.VMEM((128, 320), F32),
            pltpu.VMEM((3, 3, 320, 320), BF),
            pltpu.VMEM((6, 128, 960), BF),
        ]
        + rows_scratch
        + [pltpu.SemaphoreType.DMA((5,))],
        compiler_params=params(16),
        name="inner_rows",
    )(step_index, *near_by(merged, wide1), *stay(conv_second, time_table.T, norm_gain))

    keep, give, one, two = lax.optimization_barrier((keep, give, one, two))

    def packed(keep, give):
        got = exchange(give, plane, 1)
        return pl.pallas_call(
            pack_kernel,
            in_specs=[vmem] * 2,
            out_specs=[vmem] * 2,
            out_shape=[pair] * 2,
            compiler_params=params(2),
            name="pack",
        )(keep, got)

    def onward(i, k):
        turn = 1 if (i ^ 2) & 2 else -1
        return (((i >> 2) + turn) % planes) * GROUP + (i & 3)

    near_in, far = packed(keep, give)
    x_in = exchange(far, plane, 2)
    z_in = exchange(near_in, beside, 0)
    near_in, edge = lax.optimization_barrier((near_in, edge))

    keep, give, flat_out, weights, bias = pl.pallas_call(
        outer_kernel,
        in_specs=[smem] + [vmem] * 8 + [anywhere] * 4,
        out_specs=[vmem] * 5,
        out_shape=[
            pair, pair, chunk, pltpu.VMEM((4, 320, 320), BF), pltpu.VMEM((64, 256), F32)
        ],
        scratch_shapes=[
            pltpu.VMEM((4, 128, 960), BF),
        ]
        + rows_scratch
        + [pltpu.SemaphoreType.DMA((4,))],
        compiler_params=params(12),
        name="outer_rows",
    )(
        reach, one, two, *near_by(merged, edge, wide1, wide2, vectors), rel_bias,
        *stay(w_query, w_key, w_value, w_out),
    )

    give, x_in, z_in = lax.optimization_barrier((give, x_in, z_in))
    xz_in = exchange(x_in, onward, 0)
    near_out, far = packed(keep, give)
    x_out = exchange(far, plane, 2)
    xz_out = exchange(far, beside, 2)
    z_out = exchange(near_out, beside, 0)

    def attend(fields):
        piece = jax.ShapeDtypeStruct((128, 320), BF)
        outs = pl.pallas_call(
            attend_kernel,
            in_specs=[vmem] * 6,
            out_specs=[vmem] * 4,
            out_shape=[piece] * 4,
            scratch_shapes=[
                pltpu.VMEM((16, 64, 320), F32),
                pltpu.VMEM((16, 32, 320), BF),
                pltpu.VMEM((16, 64, 320), BF),
                pltpu.VMEM((16, 64, 320), BF),
                pltpu.VMEM((16, 64, 256), F32),
                pltpu.VMEM((16, 64, 256), BF),
                pltpu.VMEM((4, 16, 8, 320), F32),
            ],
            compiler_params=params(14),
            name="attend",
        )(*fields, *near_by(weights, bias))
        return [outs[0]] + [exchange(outs[k], plane, k) for k in (2, 3, 1)], outs[0]

    near_out, near_in = lax.optimization_barrier((near_out, near_in))
    (b0, b2, b3, b1), _ = attend((near_in, x_in, z_in, xz_in))
    back_in = [b0, b1, b2, b3]
    (b0, b2, b3, b1), mark = attend((near_out, x_out, z_out, xz_out))
    back_out = [b0, b1, b2, b3]

    def finish(first_row, second_row, back, flat, *before):
        def body(*refs):
            final_kernel(first_row, second_row, *refs)

        return pl.pallas_call(
            body,
            in_specs=[vmem] * 5 + [anywhere] * len(before),
            out_specs=anywhere,
            out_shape=jax.ShapeDtypeStruct(frames.shape, F32),
            input_output_aliases={5: 0} if before else {},
            scratch_shapes=[
                pltpu.VMEM((4, 3, 128, 128), F32),
                pltpu.VMEM((4, 8, 16, 320), F32),
                pltpu.SemaphoreType.DMA((4,)),
            ],
            compiler_params=params(6),
            name="project_out",
        )(*back, *near_by(flat), *before)

    back_in[0], mark = lax.optimization_barrier((back_in[0], mark))
    out = finish(2, 4, back_in, flat_in)
    return finish(0, 6, back_out, flat_out, out)


def solution(mesh):
    tiled = P("frame", "band", None, None)
    return jax.shard_map(
        shards, mesh=mesh, in_specs=(tiled, tiled) + (P(),) * 11, out_specs=tiled, check_vma=False
    )
```

```python
import math

import jax
import jax.numpy as jnp
from jax import lax
from jax.experimental import pallas as pl
from jax.experimental.pallas import tpu as pltpu
from jax.sharding import PartitionSpec as P

BF = jnp.bfloat16
F32 = jnp.float32
GROUP = 4
MIB = 1024 * 1024


def tapped(dst, row, tap, value):
    dst[row, :, tap * 256 : tap * 256 + 256] = value[:, :256]
    dst[row, :, 768 + tap * 64 : 832 + tap * 64] = value[:, 256:]


def arrange(dst, weight):
    for dy in range(3):
        for dx in range(3):
            w = weight[dy, dx]
            top = slice(dy * 256, dy * 256 + 256)
            low = slice(768 + dy * 64, 832 + dy * 64)
            left = slice(dx * 256, dx * 256 + 256)
            right = slice(768 + dx * 64, 832 + dx * 64)
            dst[top, left] = w[:256, :256]
            dst[top, right] = w[:256, 256:]
            dst[low, left] = w[256:, :256]
            dst[low, right] = w[256:, 256:]


def combine(prod, row):
    rows = slice(row * 128, row * 128 + 128)

    def shifted(a, b, c):
        gap = jnp.zeros((8, a.shape[1]), F32)
        return (
            b
            + jnp.concatenate([gap, a[:-8]], axis=0)
            + jnp.concatenate([c[8:], gap], axis=0)
        )

    main = shifted(prod[rows, 0:256], prod[rows, 256:512], prod[rows, 512:768])
    rest = shifted(prod[rows, 768:832], prod[rows, 832:896], prod[rows, 896:960])
    return jnp.concatenate([main, rest], axis=1)


def put(merged, row, f, value):
    value = value.astype(BF).astype(F32)
    rest = jnp.concatenate([value[:, 256:], jnp.zeros((16, 64), F32)], axis=1)
    for j, part in enumerate((value[:, :128], value[:, 128:256], rest)):
        merged[j, row, pl.ds(f, 16, stride=8), :] = part


def taken(merged, row):
    return jnp.concatenate([merged[0, row], merged[1, row], merged[2, row, :, :64]], axis=1)


def multiply(prod, taps, wide, count):
    prod[0 : count * 128, :] = jnp.dot(
        taps[...].reshape(count * 128, 960), wide[...], preferred_element_type=F32
    )


def silu(t):
    return t * (0.5 * jnp.tanh(0.5 * t) + 0.5)


def layer_norm(block, gain):
    mean = jnp.sum(block, axis=1, keepdims=True) * (1.0 / 320)
    centre = block - mean
    var = jnp.sum(centre * centre, axis=1, keepdims=True) * (1.0 / 320)
    return (centre * lax.rsqrt(var + 1e-5) * gain).astype(BF)


def bias_table(bias, rel_bias, reach):
    plane = lax.axis_index("frame") // GROUP
    line = lax.broadcasted_iota(jnp.int32, (64, 128), 0)
    lane = lax.broadcasted_iota(jnp.int32, (64, 128), 1) % 32
    limit = jnp.zeros((1, 128), jnp.int32)
    for i in range(32):
        limit = jnp.where(lane[0:1] == i, reach[plane * 32 + i], limit)
    allowed = jnp.abs(line - 16 - lane) <= limit
    padded = jnp.concatenate([rel_bias[...], jnp.zeros((8, 95), F32)], axis=1)
    for half in range(2):
        table = []
        for h in range(4 * half, 4 * half + 4):
            wide = jnp.broadcast_to(padded[h : h + 1], (32, 128))
            table.append(pltpu.roll(wide, 0, 1, stride=1, stride_axis=0))
        table = jnp.concatenate(table, axis=0).T[0:64]
        bias[:, half * 128 : half * 128 + 128] = jnp.where(
            allowed, table * (1.0 / math.log(2.0)), -jnp.inf
        )


def fold(dst, value):
    dst[0:128] = value[:, 0:128]
    dst[128:256] = value[:, 128:256]
    dst[256:320] = jnp.concatenate([value[0:64, 256:], value[64:128, 256:]], axis=1)


def unfold(value):
    rest = jnp.concatenate([value[256:320, 0:64], value[256:320, 64:128]], axis=0)
    return jnp.concatenate([value[0:128], value[128:256], rest], axis=1)


def hand_out(me, normed, keep, give):
    keep[0] = normed[me]
    keep[1] = normed[me ^ 2]
    give[0] = normed[me ^ 1]
    give[1] = normed[me ^ 3]


def in_group():
    return lax.axis_index("frame") % GROUP


def odd_band():
    return lax.axis_index("band") % 2 == 1


def merge_kernel(
    frames, control, first, one, two, rows, wide, fbuf, cbuf, buf, merged, sems
):
    loads = [
        pltpu.make_async_copy(src, dst, sems.at[i])
        for i, (src, dst) in enumerate(((frames, fbuf), (control, cbuf), (first, buf)))
    ]
    for load in loads:
        load.start()
    loads[0].wait()
    loads[1].wait()
    for m in range(8):
        for f in range(8):
            put(merged, m, f, fbuf[f, m].astype(F32) + cbuf[f, m].astype(F32))
        rows[m] = taken(merged, m).astype(BF)
    facing = jnp.where(odd_band(), 6, 0)
    for i in range(2):
        fold(one.at[i], rows[facing + i])
        fold(two.at[i], rows[6 - facing + i])
    loads[2].wait()
    arrange(wide, buf)


def inner_kernel(
    step, rows, wide1, second, table, gain,
    keep, give, flat, edge, wide2, vectors,
    line, column, tail, row, buf, taps1, taps2, prod, normed, sems,
):
    loads = [pltpu.make_async_copy(second.at[i], buf.at[i], sems.at[i]) for i in range(3)]
    load_gain = pltpu.make_async_copy(gain, line, sems.at[3])
    me = in_group()
    block = step[0] // 128
    whole_block = pltpu.make_async_copy(
        table.at[:, pl.ds(pl.multiple_of(jnp.minimum(block, 6) * 128, 128), 128)],
        column, sems.at[4],
    )
    last_block = pltpu.make_async_copy(
        table.at[:, pl.ds(896, 104)], tail, sems.at[4]
    )

    @pl.when(block < 7)
    def _():
        whole_block.start()

    @pl.when(block >= 7)
    def _():
        last_block.start()

    load_gain.start()
    for load in loads:
        load.start()
    for m in range(8):
        value = rows[m]
        for dy in range(3):
            if 0 <= m - dy < 6:
                tapped(taps1, m - dy, dy, value)
    multiply(prod, taps1, wide1, 6)

    @pl.when(block < 7)
    def _():
        whole_block.wait()
        row[...] = column[...].T

    @pl.when(block >= 7)
    def _():
        last_block.wait()
        row[0:104] = tail[...].T

    embed = row[pl.ds(step[0] % 128, 1), :]
    vectors[0:1] = embed
    load_gain.wait()
    vectors[1:2] = line[...].reshape(1, 320)
    gain = vectors[1:2]
    for r in range(6):
        act = silu(combine(prod, r) + embed).astype(BF)
        for dy in range(3):
            if 0 <= r - dy < 4:
                tapped(taps2, r - dy, dy, act)
        if r in (0, 1, 4, 5):
            edge[(0, 1, None, None, 2, 3)[r]] = act
    for load in loads:
        load.wait()
    arrange(wide2, buf)
    multiply(prod, taps2, wide2, 4)
    for y in range(4):
        value = combine(prod, y) + rows[y + 2].astype(F32)
        flat[y] = value
        fold(normed.at[y], layer_norm(value, gain))
    hand_out(me, normed, keep, give)


def outer_kernel(
    reach, one, two, merged, edge, wide1, wide2, vectors, rel_bias, wq, wk, wv, w_out,
    keep, give, flat, weights, bias,
    taps1, taps2, prod, normed, sems,
):
    loads = [
        pltpu.make_async_copy(w, weights.at[i], sems.at[i])
        for i, w in enumerate((wq, wk, wv, w_out))
    ]
    for load in loads:
        load.start()
    me = in_group()
    band = lax.axis_index("band")
    odd = odd_band()
    embed = vectors[0:1]
    gain = vectors[1:2]
    low = [unfold(jnp.where(odd, two[y], one[y])) for y in range(2)]
    high = [unfold(jnp.where(odd, one[y], two[y])) for y in range(2)]
    rows = low + [merged[0], merged[1], merged[6], merged[7]] + high
    starts = (0, 1, 4, 5)
    for m in range(8):
        for r in range(4):
            if 0 <= m - starts[r] < 3:
                tapped(taps1, r, m - starts[r], rows[m])
    multiply(prod, taps1, wide1, 4)
    act = [silu(combine(prod, r) + embed) for r in range(4)]
    act[0] = jnp.where(band == 0, 0.0, act[0])
    act[3] = jnp.where(band == lax.axis_size("band") - 1, 0.0, act[3])
    act = [a.astype(BF) for a in act]
    lines = ((act[0], act[1], edge[0], edge[1]), (edge[2], edge[3], act[2], act[3]))
    for side in range(2):
        for i in range(4):
            for dy in range(3):
                if 0 <= i - dy < 2:
                    tapped(taps2, 2 * side + i - dy, dy, lines[side][i])
    multiply(prod, taps2, wide2, 4)
    for y in range(4):
        value = combine(prod, y) + merged[(0, 1, 6, 7)[y]].astype(F32)
        flat[y] = value
        fold(normed.at[y], layer_norm(value, gain))
    hand_out(me, normed, keep, give)
    bias_table(bias, rel_bias, reach)
    for load in loads:
        load.wait()


def pack_kernel(keep, got, near, far):
    near[0] = keep[0]
    near[1] = got[0]
    far[0] = keep[1]
    far[1] = got[1]


def attend_kernel(
    near, across_x, near_z, across_z, weights, bias,
    out0, out1, out2, out3,
    field, query, key, value, score, prob, back,
):
    me = in_group()
    pixels = field.shape[0]

    for k in range(4):
        block = me ^ k
        own = (near, across_x)[k // 2]
        at = pl.multiple_of(16 + 8 * block, 8)
        field[:, pl.ds(at, 8), :] = unfold(own[k % 2].astype(F32)).reshape(pixels, 8, 320)
        halo = (near_z, across_z)[k // 2]
        at = pl.multiple_of(jnp.where(block >= 2, 8 * block - 16, 48 + 8 * block), 8)
        field[:, pl.ds(at, 8), :] = unfold(halo[k % 2].astype(F32)).reshape(pixels, 8, 320)

    def project(x, i):
        return jnp.dot(x, weights[i], preferred_element_type=F32).astype(BF)

    x = field[...].reshape(pixels * 64, 320).astype(BF)
    key[...] = project(x, 1).reshape(pixels, 64, 320)
    value[...] = project(x, 2).reshape(pixels, 64, 320)
    x = field[:, 16:48, :].reshape(pixels * 32, 320).astype(BF)
    query[...] = project(x, 0).reshape(pixels, 32, 320)

    def heads_at(lanes, base):
        lane = lax.broadcasted_iota(jnp.int32, (4, 1, lanes), 2)
        first = base + 40 * lax.broadcasted_iota(jnp.int32, (4, 1, lanes), 0)
        return ((lane >= first) & (lane < first + 40)).astype(F32).astype(BF)

    spread_low = heads_at(256, 0)
    spread_high = heads_at(192, 32)
    scale = 40.0**-0.5 / math.log(2.0)
    across = (((1,), (1,)), ((), ()))

    def scores(p):
        q = query[p]
        k = key[p]
        low = (q[None, :, 0:256] * spread_low).reshape(128, 256)
        high = (q[None, :, 128:320] * spread_high).reshape(128, 192)
        score[p, :, 0:128] = lax.dot_general(
            k[:, 0:256], low, across, preferred_element_type=F32
        )
        score[p, :, 128:256] = lax.dot_general(
            k[:, 128:320], high, across, preferred_element_type=F32
        )

    def softmax(p):
        s = score[p] * scale + bias[...]
        e = jnp.exp2(s - jnp.max(s, axis=0, keepdims=True))
        prob[p] = (e * (1.0 / jnp.sum(e, axis=0, keepdims=True))).astype(BF)

    def inside(h, lanes, base):
        lane = lax.broadcasted_iota(jnp.int32, (1, lanes), 1) + base
        return (lane >= 40 * h) & (lane < 40 * h + 40)

    def attended(p):
        w = prob[p].T
        v = value[p]
        low = jnp.dot(w[0:128], v[:, 0:256], preferred_element_type=F32)
        high = jnp.dot(w[128:256], v[:, 128:320], preferred_element_type=F32)
        left = low[0:32, 0:128]
        for h in (1, 2, 3):
            left = jnp.where(inside(h, 128, 0), low[32 * h : 32 * h + 32, 0:128], left)
        middle = low[96:128, 128:256]
        for h in (4, 5, 6):
            at = 32 * h - 128
            middle = jnp.where(inside(h, 128, 128), high[at : at + 32, 0:128], middle)
        right = jnp.where(inside(7, 64, 256), high[96:128, 128:192], high[64:96, 128:192])
        att = jnp.concatenate([left, middle, right], axis=1)
        for b in range(4):
            back[b, p] = att[8 * b : 8 * b + 8]

    def each(step):
        def some(i, carry):
            for j in range(16):
                step(i * 16 + j)
            return carry

        lax.fori_loop(0, pixels // 16, some, 0)

    each(scores)
    each(softmax)
    each(attended)
    for k, out in enumerate((out0, out1, out2, out3)):
        fold(out, project(back[me ^ k].reshape(pixels * 8, 320).astype(BF), 3))


def final_kernel(first_row, second_row, *refs):
    a0, a1, a2, a3, flat = refs[:5]
    me = in_group()
    out, total, done, sems = refs[-4:]
    stores = []
    for k, a in enumerate((a0, a1, a2, a3)):
        q = me ^ k
        row = jnp.where(q >= 2, second_row + q - 2, first_row + q)
        value = unfold(a[...].astype(F32)) + flat[q]
        rest = jnp.concatenate([value[:, 256:], jnp.zeros((128, 64), F32)], axis=1)
        for j, part in enumerate((value[:, :128], value[:, 128:256], rest)):
            total[k, j] = part
        for f in range(8):
            for j, width in enumerate((128, 128, 64)):
                part = total[k, j, pl.ds(f, 16, stride=8), :]
                done[k, f, :, j * 128 : j * 128 + width] = part[:, :width]
        store = pltpu.make_async_copy(done.at[k], out.at[:, row], sems.at[k])
        store.start()
        stores.append(store)
    for store in stores:
        store.wait()


def shards(
    frames, control, conv_first, conv_second, time_table, step_index, norm_gain,
    w_query, w_key, w_value, w_out, rel_bias, reach,
):
    count = lax.axis_size("frame")
    bands = lax.axis_size("band")
    planes = count // GROUP
    def swaps(first):
        pairs = [(i, i + 1) for i in range(first, bands - 1, 2)]
        return pairs + [(j, i) for i, j in pairs]

    def plane(i, k):
        return (i & ~3) | ((i & 3) ^ k)

    def beside(i, k):
        turn = 1 if i & 2 else -1
        return (((i >> 2) + turn) % planes) * GROUP + ((i & 3) ^ k)

    def exchange(x, to, k):
        return lax.ppermute(x, "frame", [(i, to(i, k)) for i in range(count)])

    vmem = pl.BlockSpec(memory_space=pltpu.VMEM)
    smem = pl.BlockSpec(memory_space=pltpu.SMEM)
    anywhere = pl.BlockSpec(memory_space=pltpu.HBM)

    def params(mebibytes):
        return pltpu.CompilerParams(vmem_limit_bytes=mebibytes * MIB)
    pair = jax.ShapeDtypeStruct((2, 320, 128), BF)
    chunk = pltpu.VMEM((4, 128, 320), F32)

    def cost(flops):
        return pl.CostEstimate(flops=flops, bytes_accessed=4_000_000, transcendentals=0)

    def stay(*arrays):
        return [pltpu.with_memory_space_constraint(x, pltpu.HBM) for x in arrays]

    def near_by(*arrays):
        return [pltpu.with_memory_space_constraint(x, pltpu.VMEM) for x in arrays]

    rows_scratch = [
        pltpu.VMEM((4, 128, 960), BF),
        pltpu.VMEM((768, 960), F32),
        pltpu.VMEM((4, 320, 128), BF),
    ]
    wide = pltpu.VMEM((960, 960), BF)
    one, two, merged, wide1 = pl.pallas_call(
        merge_kernel,
        in_specs=[anywhere] * 3,
        out_specs=[vmem] * 4,
        out_shape=[pair, pair, pltpu.VMEM((8, 128, 320), BF), wide],
        scratch_shapes=[
            pltpu.VMEM((8, 8, 16, 320), BF),
            pltpu.VMEM((8, 8, 16, 320), BF),
            pltpu.VMEM((3, 3, 320, 320), BF),
            pltpu.VMEM((3, 8, 128, 128), F32),
            pltpu.SemaphoreType.DMA((3,)),
        ],
        compiler_params=params(8),
        name="merge",
    )(*stay(frames, control, conv_first))
    one, two, step_index = lax.optimization_barrier((one, two, step_index))
    one = lax.ppermute(one, "band", swaps(1))
    two = lax.ppermute(two, "band", swaps(0))

    keep, give, flat_in, edge, wide2, vectors = pl.pallas_call(
        inner_kernel,
        in_specs=[smem] + [vmem] * 2 + [anywhere] * 3,
        out_specs=[vmem] * 6,
        out_shape=[
            pair, pair, chunk, pltpu.VMEM((4, 128, 320), BF), wide, pltpu.VMEM((2, 320), F32)
        ],
        scratch_shapes=[
            pltpu.VMEM((320,), F32),
            pltpu.VMEM((320, 128), F32),
            pltpu.VMEM((320, 104), F32),
            pltpu.VMEM((128, 320), F32),
            pltpu.VMEM((3, 3, 320, 320), BF),
            pltpu.VMEM((6, 128, 960), BF),
        ]
        + rows_scratch
        + [pltpu.SemaphoreType.DMA((5,))],
        compiler_params=params(16),
        name="inner_rows",
    )(step_index, *near_by(merged, wide1), *stay(conv_second, time_table.T, norm_gain))

    keep, give, one, two = lax.optimization_barrier((keep, give, one, two))

    def packed(keep, give):
        got = exchange(give, plane, 1)
        return pl.pallas_call(
            pack_kernel,
            in_specs=[vmem] * 2,
            out_specs=[vmem] * 2,
            out_shape=[pair] * 2,
            compiler_params=params(2),
            name="pack",
        )(keep, got)

    def onward(i, k):
        turn = 1 if (i ^ 2) & 2 else -1
        return (((i >> 2) + turn) % planes) * GROUP + (i & 3)

    near_in, far = packed(keep, give)
    x_in = exchange(far, plane, 2)
    z_in = exchange(near_in, beside, 0)
    near_in, edge = lax.optimization_barrier((near_in, edge))

    keep, give, flat_out, weights, bias = pl.pallas_call(
        outer_kernel,
        in_specs=[smem] + [vmem] * 8 + [anywhere] * 4,
        out_specs=[vmem] * 5,
        out_shape=[
            pair, pair, chunk, pltpu.VMEM((4, 320, 320), BF), pltpu.VMEM((64, 256), F32)
        ],
        scratch_shapes=[
            pltpu.VMEM((4, 128, 960), BF),
        ]
        + rows_scratch
        + [pltpu.SemaphoreType.DMA((4,))],
        compiler_params=params(12),
        name="outer_rows",
    )(
        reach, one, two, *near_by(merged, edge, wide1, wide2, vectors), rel_bias,
        *stay(w_query, w_key, w_value, w_out),
    )

    give, x_in, z_in = lax.optimization_barrier((give, x_in, z_in))
    xz_in = exchange(x_in, onward, 0)
    near_out, far = packed(keep, give)
    x_out = exchange(far, plane, 2)
    xz_out = exchange(far, beside, 2)
    z_out = exchange(near_out, beside, 0)

    def attend(fields):
        piece = jax.ShapeDtypeStruct((320, 128), BF)
        outs = pl.pallas_call(
            attend_kernel,
            in_specs=[vmem] * 6,
            out_specs=[vmem] * 4,
            out_shape=[piece] * 4,
            scratch_shapes=[
                pltpu.VMEM((16, 64, 320), F32),
                pltpu.VMEM((16, 32, 320), BF),
                pltpu.VMEM((16, 64, 320), BF),
                pltpu.VMEM((16, 64, 320), BF),
                pltpu.VMEM((16, 64, 256), F32),
                pltpu.VMEM((16, 64, 256), BF),
                pltpu.VMEM((4, 16, 8, 320), F32),
            ],
            compiler_params=params(14),
            name="attend",
        )(*fields, *near_by(weights, bias))
        return [outs[0]] + [exchange(outs[k], plane, k) for k in (2, 3, 1)], outs[0]

    near_out, near_in = lax.optimization_barrier((near_out, near_in))
    (b0, b2, b3, b1), _ = attend((near_in, x_in, z_in, xz_in))
    back_in = [b0, b1, b2, b3]
    (b0, b2, b3, b1), mark = attend((near_out, x_out, z_out, xz_out))
    back_out = [b0, b1, b2, b3]

    def finish(first_row, second_row, back, flat, *before):
        def body(*refs):
            final_kernel(first_row, second_row, *refs)

        return pl.pallas_call(
            body,
            in_specs=[vmem] * 5 + [anywhere] * len(before),
            out_specs=anywhere,
            out_shape=jax.ShapeDtypeStruct(frames.shape, F32),
            input_output_aliases={5: 0} if before else {},
            scratch_shapes=[
                pltpu.VMEM((4, 3, 128, 128), F32),
                pltpu.VMEM((4, 8, 16, 320), F32),
                pltpu.SemaphoreType.DMA((4,)),
            ],
            compiler_params=params(6),
            name="project_out",
        )(*back, *near_by(flat), *before)

    back_in[0], mark = lax.optimization_barrier((back_in[0], mark))
    out = finish(2, 4, back_in, flat_in)
    return finish(0, 6, back_out, flat_out, out)


def solution(mesh):
    tiled = P("frame", "band", None, None)
    return jax.shard_map(
        shards, mesh=mesh, in_specs=(tiled, tiled) + (P(),) * 11, out_specs=tiled, check_vma=False
    )
```

```python
import math

import jax
import jax.numpy as jnp
from jax import lax
from jax.experimental import pallas as pl
from jax.experimental.pallas import tpu as pltpu
from jax.sharding import PartitionSpec as P

BF = jnp.bfloat16
F32 = jnp.float32
GROUP = 4
MIB = 1024 * 1024


def tapped(dst, row, tap, value):
    dst[row, :, tap * 256 : tap * 256 + 256] = value[:, :256]
    dst[row, :, 768 + tap * 64 : 832 + tap * 64] = value[:, 256:]


def arrange(dst, weight):
    for dy in range(3):
        for dx in range(3):
            w = weight[dy, dx]
            top = slice(dy * 256, dy * 256 + 256)
            low = slice(768 + dy * 64, 832 + dy * 64)
            left = slice(dx * 256, dx * 256 + 256)
            right = slice(768 + dx * 64, 832 + dx * 64)
            dst[top, left] = w[:256, :256]
            dst[top, right] = w[:256, 256:]
            dst[low, left] = w[256:, :256]
            dst[low, right] = w[256:, 256:]


def combine(prod, row):
    rows = slice(row * 128, row * 128 + 128)

    def shifted(a, b, c):
        gap = jnp.zeros((8, a.shape[1]), F32)
        return (
            b
            + jnp.concatenate([gap, a[:-8]], axis=0)
            + jnp.concatenate([c[8:], gap], axis=0)
        )

    main = shifted(prod[rows, 0:256], prod[rows, 256:512], prod[rows, 512:768])
    rest = shifted(prod[rows, 768:832], prod[rows, 832:896], prod[rows, 896:960])
    return jnp.concatenate([main, rest], axis=1)


def put(merged, row, f, value):
    value = value.astype(BF).astype(F32)
    rest = jnp.concatenate([value[:, 256:], jnp.zeros((16, 64), F32)], axis=1)
    for j, part in enumerate((value[:, :128], value[:, 128:256], rest)):
        merged[j, row, pl.ds(f, 16, stride=8), :] = part


def taken(merged, row):
    return jnp.concatenate([merged[0, row], merged[1, row], merged[2, row, :, :64]], axis=1)


def multiply(prod, taps, wide, count):
    prod[0 : count * 128, :] = jnp.dot(
        taps[...].reshape(count * 128, 960), wide[...], preferred_element_type=F32
    )


def silu(t):
    return t * (0.5 * jnp.tanh(0.5 * t) + 0.5)


def layer_norm(block, gain):
    mean = jnp.sum(block, axis=1, keepdims=True) * (1.0 / 320)
    centre = block - mean
    var = jnp.sum(centre * centre, axis=1, keepdims=True) * (1.0 / 320)
    return (centre * lax.rsqrt(var + 1e-5) * gain).astype(BF)


def bias_table(bias, rel_bias, reach):
    plane = lax.axis_index("frame") // GROUP
    line = lax.broadcasted_iota(jnp.int32, (64, 128), 0)
    lane = lax.broadcasted_iota(jnp.int32, (64, 128), 1) % 32
    limit = jnp.zeros((1, 128), jnp.int32)
    for i in range(32):
        limit = jnp.where(lane[0:1] == i, reach[plane * 32 + i], limit)
    allowed = jnp.abs(line - 16 - lane) <= limit
    padded = jnp.concatenate([rel_bias[...], jnp.zeros((8, 95), F32)], axis=1)
    for half in range(2):
        table = []
        for h in range(4 * half, 4 * half + 4):
            wide = jnp.broadcast_to(padded[h : h + 1], (32, 128))
            table.append(pltpu.roll(wide, 0, 1, stride=1, stride_axis=0))
        table = jnp.concatenate(table, axis=0).T[0:64]
        bias[:, half * 128 : half * 128 + 128] = jnp.where(
            allowed, table * (1.0 / math.log(2.0)), -jnp.inf
        )


def fold(dst, value):
    dst[0:128] = value[:, 0:128]
    dst[128:256] = value[:, 128:256]
    dst[256:320] = jnp.concatenate([value[0:64, 256:], value[64:128, 256:]], axis=1)


def unfold(value):
    rest = jnp.concatenate([value[256:320, 0:64], value[256:320, 64:128]], axis=0)
    return jnp.concatenate([value[0:128], value[128:256], rest], axis=1)


def hand_out(me, normed, keep, give):
    keep[0] = normed[me]
    keep[1] = normed[me ^ 2]
    give[0] = normed[me ^ 1]
    give[1] = normed[me ^ 3]


def in_group():
    return lax.axis_index("frame") % GROUP


def odd_band():
    return lax.axis_index("band") % 2 == 1


def merge_kernel(
    step, frames, control, table, gain, one, two, rows, vectors,
    line, column, tail, row, fbuf, cbuf, merged, sems,
):
    loads = [
        pltpu.make_async_copy(src, dst, sems.at[i])
        for i, (src, dst) in enumerate(((frames, fbuf), (control, cbuf), (gain, line)))
    ]
    for load in loads:
        load.start()
    block = step[0] // 128
    whole_block = pltpu.make_async_copy(
        table.at[:, pl.ds(pl.multiple_of(jnp.minimum(block, 6) * 128, 128), 128)],
        column, sems.at[3],
    )
    last_block = pltpu.make_async_copy(
        table.at[:, pl.ds(896, 104)], tail, sems.at[3]
    )

    @pl.when(block < 7)
    def _():
        whole_block.start()

    @pl.when(block >= 7)
    def _():
        last_block.start()

    loads[0].wait()
    loads[1].wait()
    for m in range(8):
        for f in range(8):
            put(merged, m, f, fbuf[f, m].astype(F32) + cbuf[f, m].astype(F32))
        rows[m] = taken(merged, m).astype(BF)
    facing = jnp.where(odd_band(), 6, 0)
    for i in range(2):
        fold(one.at[i], rows[facing + i])
        fold(two.at[i], rows[6 - facing + i])

    @pl.when(block < 7)
    def _():
        whole_block.wait()
        row[...] = column[...].T

    @pl.when(block >= 7)
    def _():
        last_block.wait()
        row[0:104] = tail[...].T

    vectors[0:1] = row[pl.ds(step[0] % 128, 1), :]
    loads[2].wait()
    vectors[1:2] = line[...].reshape(1, 320)


def inner_kernel(
    rows, first, second, vectors,
    keep, give, flat, edge, wide1, wide2,
    buf, taps1, taps2, prod, normed, sems,
):
    loads = [pltpu.make_async_copy(second.at[i], buf.at[i], sems.at[i]) for i in range(3)]
    for load in loads:
        load.start()
    me = in_group()
    for m in range(8):
        value = rows[m]
        for dy in range(3):
            if 0 <= m - dy < 6:
                tapped(taps1, m - dy, dy, value)
    arrange(wide1, first)
    multiply(prod, taps1, wide1, 6)

    embed = vectors[0:1]
    gain = vectors[1:2]
    for r in range(6):
        act = silu(combine(prod, r) + embed).astype(BF)
        for dy in range(3):
            if 0 <= r - dy < 4:
                tapped(taps2, r - dy, dy, act)
        if r in (0, 1, 4, 5):
            edge[(0, 1, None, None, 2, 3)[r]] = act
    for load in loads:
        load.wait()
    arrange(wide2, buf)
    multiply(prod, taps2, wide2, 4)
    for y in range(4):
        value = combine(prod, y) + rows[y + 2].astype(F32)
        flat[y] = value
        fold(normed.at[y], layer_norm(value, gain))
    hand_out(me, normed, keep, give)


def outer_kernel(
    reach, one, two, merged, edge, wide1, wide2, vectors, rel_bias, wq, wk, wv, w_out,
    keep, give, flat, weights, bias,
    taps1, taps2, prod, normed, sems,
):
    loads = [
        pltpu.make_async_copy(w, weights.at[i], sems.at[i])
        for i, w in enumerate((wq, wk, wv, w_out))
    ]
    for load in loads:
        load.start()
    me = in_group()
    band = lax.axis_index("band")
    odd = odd_band()
    embed = vectors[0:1]
    gain = vectors[1:2]
    low = [unfold(jnp.where(odd, two[y], one[y])) for y in range(2)]
    high = [unfold(jnp.where(odd, one[y], two[y])) for y in range(2)]
    rows = low + [merged[0], merged[1], merged[6], merged[7]] + high
    starts = (0, 1, 4, 5)
    for m in range(8):
        for r in range(4):
            if 0 <= m - starts[r] < 3:
                tapped(taps1, r, m - starts[r], rows[m])
    multiply(prod, taps1, wide1, 4)
    act = [silu(combine(prod, r) + embed) for r in range(4)]
    act[0] = jnp.where(band == 0, 0.0, act[0])
    act[3] = jnp.where(band == lax.axis_size("band") - 1, 0.0, act[3])
    act = [a.astype(BF) for a in act]
    lines = ((act[0], act[1], edge[0], edge[1]), (edge[2], edge[3], act[2], act[3]))
    for side in range(2):
        for i in range(4):
            for dy in range(3):
                if 0 <= i - dy < 2:
                    tapped(taps2, 2 * side + i - dy, dy, lines[side][i])
    multiply(prod, taps2, wide2, 4)
    for y in range(4):
        value = combine(prod, y) + merged[(0, 1, 6, 7)[y]].astype(F32)
        flat[y] = value
        fold(normed.at[y], layer_norm(value, gain))
    hand_out(me, normed, keep, give)
    bias_table(bias, rel_bias, reach)
    for load in loads:
        load.wait()


def pack_kernel(keep, got, near, far):
    near[0] = keep[0]
    near[1] = got[0]
    far[0] = keep[1]
    far[1] = got[1]


def attend_kernel(
    near, across_x, near_z, across_z, weights, bias,
    out0, out1, out2, out3,
    field, query, key, value, score, prob, back,
):
    me = in_group()
    pixels = field.shape[0]

    for k in range(4):
        block = me ^ k
        own = (near, across_x)[k // 2]
        at = pl.multiple_of(16 + 8 * block, 8)
        field[:, pl.ds(at, 8), :] = unfold(own[k % 2].astype(F32)).reshape(pixels, 8, 320)
        halo = (near_z, across_z)[k // 2]
        at = pl.multiple_of(jnp.where(block >= 2, 8 * block - 16, 48 + 8 * block), 8)
        field[:, pl.ds(at, 8), :] = unfold(halo[k % 2].astype(F32)).reshape(pixels, 8, 320)

    def project(x, i):
        return jnp.dot(x, weights[i], preferred_element_type=F32).astype(BF)

    x = field[...].reshape(pixels * 64, 320).astype(BF)
    key[...] = project(x, 1).reshape(pixels, 64, 320)
    value[...] = project(x, 2).reshape(pixels, 64, 320)
    x = field[:, 16:48, :].reshape(pixels * 32, 320).astype(BF)
    query[...] = project(x, 0).reshape(pixels, 32, 320)

    def heads_at(lanes, base):
        lane = lax.broadcasted_iota(jnp.int32, (4, 1, lanes), 2)
        first = base + 40 * lax.broadcasted_iota(jnp.int32, (4, 1, lanes), 0)
        return ((lane >= first) & (lane < first + 40)).astype(F32).astype(BF)

    spread_low = heads_at(256, 0)
    spread_high = heads_at(192, 32)
    scale = 40.0**-0.5 / math.log(2.0)
    across = (((1,), (1,)), ((), ()))

    def scores(p):
        q = query[p]
        k = key[p]
        low = (q[None, :, 0:256] * spread_low).reshape(128, 256)
        high = (q[None, :, 128:320] * spread_high).reshape(128, 192)
        score[p, :, 0:128] = lax.dot_general(
            k[:, 0:256], low, across, preferred_element_type=F32
        )
        score[p, :, 128:256] = lax.dot_general(
            k[:, 128:320], high, across, preferred_element_type=F32
        )

    def softmax(p):
        s = score[p] * scale + bias[...]
        e = jnp.exp2(s - jnp.max(s, axis=0, keepdims=True))
        prob[p] = (e * (1.0 / jnp.sum(e, axis=0, keepdims=True))).astype(BF)

    def inside(h, lanes, base):
        lane = lax.broadcasted_iota(jnp.int32, (1, lanes), 1) + base
        return (lane >= 40 * h) & (lane < 40 * h + 40)

    def attended(p):
        w = prob[p].T
        v = value[p]
        low = jnp.dot(w[0:128], v[:, 0:256], preferred_element_type=F32)
        high = jnp.dot(w[128:256], v[:, 128:320], preferred_element_type=F32)
        left = low[0:32, 0:128]
        for h in (1, 2, 3):
            left = jnp.where(inside(h, 128, 0), low[32 * h : 32 * h + 32, 0:128], left)
        middle = low[96:128, 128:256]
        for h in (4, 5, 6):
            at = 32 * h - 128
            middle = jnp.where(inside(h, 128, 128), high[at : at + 32, 0:128], middle)
        right = jnp.where(inside(7, 64, 256), high[96:128, 128:192], high[64:96, 128:192])
        att = jnp.concatenate([left, middle, right], axis=1)
        for b in range(4):
            back[b, p] = att[8 * b : 8 * b + 8]

    def each(step):
        def some(i, carry):
            for j in range(16):
                step(i * 16 + j)
            return carry

        lax.fori_loop(0, pixels // 16, some, 0)

    each(scores)
    each(softmax)
    each(attended)
    for k, out in enumerate((out0, out1, out2, out3)):
        fold(out, project(back[me ^ k].reshape(pixels * 8, 320).astype(BF), 3))


def final_kernel(first_row, second_row, *refs):
    a0, a1, a2, a3, flat = refs[:5]
    me = in_group()
    out, total, done, sems = refs[-4:]
    stores = []
    for k, a in enumerate((a0, a1, a2, a3)):
        q = me ^ k
        row = jnp.where(q >= 2, second_row + q - 2, first_row + q)
        value = unfold(a[...].astype(F32)) + flat[q]
        rest = jnp.concatenate([value[:, 256:], jnp.zeros((128, 64), F32)], axis=1)
        for j, part in enumerate((value[:, :128], value[:, 128:256], rest)):
            total[k, j] = part
        for f in range(8):
            for j, width in enumerate((128, 128, 64)):
                part = total[k, j, pl.ds(f, 16, stride=8), :]
                done[k, f, :, j * 128 : j * 128 + width] = part[:, :width]
        store = pltpu.make_async_copy(done.at[k], out.at[:, row], sems.at[k])
        store.start()
        stores.append(store)
    for store in stores:
        store.wait()


def shards(
    frames, control, conv_first, conv_second, time_table, step_index, norm_gain,
    w_query, w_key, w_value, w_out, rel_bias, reach,
):
    count = lax.axis_size("frame")
    bands = lax.axis_size("band")
    planes = count // GROUP
    def swaps(first):
        pairs = [(i, i + 1) for i in range(first, bands - 1, 2)]
        return pairs + [(j, i) for i, j in pairs]

    def plane(i, k):
        return (i & ~3) | ((i & 3) ^ k)

    def beside(i, k):
        turn = 1 if i & 2 else -1
        return (((i >> 2) + turn) % planes) * GROUP + ((i & 3) ^ k)

    def exchange(x, to, k):
        return lax.ppermute(x, "frame", [(i, to(i, k)) for i in range(count)])

    vmem = pl.BlockSpec(memory_space=pltpu.VMEM)
    smem = pl.BlockSpec(memory_space=pltpu.SMEM)
    anywhere = pl.BlockSpec(memory_space=pltpu.HBM)

    def params(mebibytes):
        return pltpu.CompilerParams(vmem_limit_bytes=mebibytes * MIB)
    pair = jax.ShapeDtypeStruct((2, 320, 128), BF)
    chunk = pltpu.VMEM((4, 128, 320), F32)

    def cost(flops):
        return pl.CostEstimate(flops=flops, bytes_accessed=4_000_000, transcendentals=0)

    def stay(*arrays):
        return [pltpu.with_memory_space_constraint(x, pltpu.HBM) for x in arrays]

    def near_by(*arrays):
        return [pltpu.with_memory_space_constraint(x, pltpu.VMEM) for x in arrays]

    rows_scratch = [
        pltpu.VMEM((4, 128, 960), BF),
        pltpu.VMEM((768, 960), F32),
        pltpu.VMEM((4, 320, 128), BF),
    ]
    wide = pltpu.VMEM((960, 960), BF)
    one, two, merged, vectors = pl.pallas_call(
        merge_kernel,
        in_specs=[smem] + [anywhere] * 4,
        out_specs=[vmem] * 4,
        out_shape=[pair, pair, pltpu.VMEM((8, 128, 320), BF), pltpu.VMEM((2, 320), F32)],
        scratch_shapes=[
            pltpu.VMEM((320,), F32),
            pltpu.VMEM((320, 128), F32),
            pltpu.VMEM((320, 104), F32),
            pltpu.VMEM((128, 320), F32),
            pltpu.VMEM((8, 8, 16, 320), BF),
            pltpu.VMEM((8, 8, 16, 320), BF),
            pltpu.VMEM((3, 8, 128, 128), F32),
            pltpu.SemaphoreType.DMA((4,)),
        ],
        compiler_params=params(8),
        name="merge",
    )(step_index, *stay(frames, control, time_table.T, norm_gain))
    one, two, vectors = lax.optimization_barrier((one, two, vectors))
    one = lax.ppermute(one, "band", swaps(1))
    two = lax.ppermute(two, "band", swaps(0))

    first = exchange(conv_first, plane, 1)
    keep, give, flat_in, edge, wide1, wide2 = pl.pallas_call(
        inner_kernel,
        in_specs=[vmem] * 2 + [anywhere, vmem],
        out_specs=[vmem] * 6,
        out_shape=[pair, pair, chunk, pltpu.VMEM((4, 128, 320), BF), wide, wide],
        scratch_shapes=[
            pltpu.VMEM((3, 3, 320, 320), BF),
            pltpu.VMEM((6, 128, 960), BF),
        ]
        + rows_scratch
        + [pltpu.SemaphoreType.DMA((3,))],
        compiler_params=params(16),
        name="inner_rows",
    )(*near_by(merged, first), *stay(conv_second), *near_by(vectors))

    keep, give, one, two = lax.optimization_barrier((keep, give, one, two))

    def packed(keep, give):
        got = exchange(give, plane, 1)
        return pl.pallas_call(
            pack_kernel,
            in_specs=[vmem] * 2,
            out_specs=[vmem] * 2,
            out_shape=[pair] * 2,
            compiler_params=params(2),
            name="pack",
        )(keep, got)

    def onward(i, k):
        turn = 1 if (i ^ 2) & 2 else -1
        return (((i >> 2) + turn) % planes) * GROUP + (i & 3)

    near_in, far = packed(keep, give)
    x_in = exchange(far, plane, 2)
    z_in = exchange(near_in, beside, 0)
    near_in, edge = lax.optimization_barrier((near_in, edge))

    keep, give, flat_out, weights, bias = pl.pallas_call(
        outer_kernel,
        in_specs=[smem] + [vmem] * 8 + [anywhere] * 4,
        out_specs=[vmem] * 5,
        out_shape=[
            pair, pair, chunk, pltpu.VMEM((4, 320, 320), BF), pltpu.VMEM((64, 256), F32)
        ],
        scratch_shapes=[
            pltpu.VMEM((4, 128, 960), BF),
        ]
        + rows_scratch
        + [pltpu.SemaphoreType.DMA((4,))],
        compiler_params=params(12),
        name="outer_rows",
    )(
        reach, one, two, *near_by(merged, edge, wide1, wide2, vectors), rel_bias,
        *stay(w_query, w_key, w_value, w_out),
    )

    give, x_in, z_in = lax.optimization_barrier((give, x_in, z_in))
    xz_in = exchange(x_in, onward, 0)
    near_out, far = packed(keep, give)
    x_out = exchange(far, plane, 2)
    xz_out = exchange(far, beside, 2)
    z_out = exchange(near_out, beside, 0)

    def attend(fields):
        piece = jax.ShapeDtypeStruct((320, 128), BF)
        outs = pl.pallas_call(
            attend_kernel,
            in_specs=[vmem] * 6,
            out_specs=[vmem] * 4,
            out_shape=[piece] * 4,
            scratch_shapes=[
                pltpu.VMEM((16, 64, 320), F32),
                pltpu.VMEM((16, 32, 320), BF),
                pltpu.VMEM((16, 64, 320), BF),
                pltpu.VMEM((16, 64, 320), BF),
                pltpu.VMEM((16, 64, 256), F32),
                pltpu.VMEM((16, 64, 256), BF),
                pltpu.VMEM((4, 16, 8, 320), F32),
            ],
            compiler_params=params(14),
            name="attend",
        )(*fields, *near_by(weights, bias))
        return [outs[0]] + [exchange(outs[k], plane, k) for k in (2, 3, 1)], outs[0]

    near_out, near_in = lax.optimization_barrier((near_out, near_in))
    (b0, b2, b3, b1), _ = attend((near_in, x_in, z_in, xz_in))
    back_in = [b0, b1, b2, b3]
    (b0, b2, b3, b1), mark = attend((near_out, x_out, z_out, xz_out))
    back_out = [b0, b1, b2, b3]

    def finish(first_row, second_row, back, flat, *before):
        def body(*refs):
            final_kernel(first_row, second_row, *refs)

        return pl.pallas_call(
            body,
            in_specs=[vmem] * 5 + [anywhere] * len(before),
            out_specs=anywhere,
            out_shape=jax.ShapeDtypeStruct(frames.shape, F32),
            input_output_aliases={5: 0} if before else {},
            scratch_shapes=[
                pltpu.VMEM((4, 3, 128, 128), F32),
                pltpu.VMEM((4, 8, 16, 320), F32),
                pltpu.SemaphoreType.DMA((4,)),
            ],
            compiler_params=params(6),
            name="project_out",
        )(*back, *near_by(flat), *before)

    back_in[0], mark = lax.optimization_barrier((back_in[0], mark))
    out = finish(2, 4, back_in, flat_in)
    return finish(0, 6, back_out, flat_out, out)


def solution(mesh):
    tiled = P("frame", "band", None, None)
    return jax.shard_map(
        shards, mesh=mesh, in_specs=(tiled, tiled) + (P(),) * 11, out_specs=tiled, check_vma=False
    )
```

```python
import math

import jax
import jax.numpy as jnp
from jax import lax
from jax.experimental import pallas as pl
from jax.experimental.pallas import tpu as pltpu
from jax.sharding import PartitionSpec as P

BF = jnp.bfloat16
F32 = jnp.float32
GROUP = 4
MIB = 1024 * 1024


def tapped(dst, row, tap, value):
    dst[row, :, tap * 256 : tap * 256 + 256] = value[:, :256]
    dst[row, :, 768 + tap * 64 : 832 + tap * 64] = value[:, 256:]


def arrange(dst, weight):
    for dy in range(3):
        for dx in range(3):
            w = weight[dy, dx]
            top = slice(dy * 256, dy * 256 + 256)
            low = slice(768 + dy * 64, 832 + dy * 64)
            left = slice(dx * 256, dx * 256 + 256)
            right = slice(768 + dx * 64, 832 + dx * 64)
            dst[top, left] = w[:256, :256]
            dst[top, right] = w[:256, 256:]
            dst[low, left] = w[256:, :256]
            dst[low, right] = w[256:, 256:]


def combine(prod, row):
    rows = slice(row * 128, row * 128 + 128)

    def shifted(a, b, c):
        gap = jnp.zeros((8, a.shape[1]), F32)
        return (
            b
            + jnp.concatenate([gap, a[:-8]], axis=0)
            + jnp.concatenate([c[8:], gap], axis=0)
        )

    main = shifted(prod[rows, 0:256], prod[rows, 256:512], prod[rows, 512:768])
    rest = shifted(prod[rows, 768:832], prod[rows, 832:896], prod[rows, 896:960])
    return jnp.concatenate([main, rest], axis=1)


def put(merged, row, f, value):
    value = value.astype(BF).astype(F32)
    rest = jnp.concatenate([value[:, 256:], jnp.zeros((16, 64), F32)], axis=1)
    for j, part in enumerate((value[:, :128], value[:, 128:256], rest)):
        merged[j, row, pl.ds(f, 16, stride=8), :] = part


def taken(merged, row):
    return jnp.concatenate([merged[0, row], merged[1, row], merged[2, row, :, :64]], axis=1)


def multiply(prod, taps, wide, count):
    prod[0 : count * 128, :] = jnp.dot(
        taps[...].reshape(count * 128, 960), wide[...], preferred_element_type=F32
    )


def silu(t):
    return t * (0.5 * jnp.tanh(0.5 * t) + 0.5)


def layer_norm(block, gain):
    mean = jnp.sum(block, axis=1, keepdims=True) * (1.0 / 320)
    centre = block - mean
    var = jnp.sum(centre * centre, axis=1, keepdims=True) * (1.0 / 320)
    return (centre * lax.rsqrt(var + 1e-5) * gain).astype(BF)


def bias_table(bias, rel_bias, reach):
    plane = lax.axis_index("frame") // GROUP
    line = lax.broadcasted_iota(jnp.int32, (64, 128), 0)
    lane = lax.broadcasted_iota(jnp.int32, (64, 128), 1) % 32
    limit = jnp.zeros((1, 128), jnp.int32)
    for i in range(32):
        limit = jnp.where(lane[0:1] == i, reach[plane * 32 + i], limit)
    allowed = jnp.abs(line - 16 - lane) <= limit
    padded = jnp.concatenate([rel_bias[...], jnp.zeros((8, 95), F32)], axis=1)
    for half in range(2):
        table = []
        for h in range(4 * half, 4 * half + 4):
            wide = jnp.broadcast_to(padded[h : h + 1], (32, 128))
            table.append(pltpu.roll(wide, 0, 1, stride=1, stride_axis=0))
        table = jnp.concatenate(table, axis=0).T[0:64]
        bias[:, half * 128 : half * 128 + 128] = jnp.where(
            allowed, table * (1.0 / math.log(2.0)), -jnp.inf
        )


def fold(dst, value):
    dst[0:128] = value[:, 0:128]
    dst[128:256] = value[:, 128:256]
    dst[256:320] = jnp.concatenate([value[0:64, 256:], value[64:128, 256:]], axis=1)


def unfold(value):
    rest = jnp.concatenate([value[256:320, 0:64], value[256:320, 64:128]], axis=0)
    return jnp.concatenate([value[0:128], value[128:256], rest], axis=1)


def hand_out(me, normed, keep, give):
    keep[0] = normed[me]
    keep[1] = normed[me ^ 2]
    give[0] = normed[me ^ 1]
    give[1] = normed[me ^ 3]


def in_group():
    return lax.axis_index("frame") % GROUP


def odd_band():
    return lax.axis_index("band") % 2 == 1


def merge_kernel(
    step, frames, control, table, gain, one, two, rows, vectors,
    line, column, tail, row, fbuf, cbuf, merged, sems,
):
    loads = [
        pltpu.make_async_copy(src, dst, sems.at[i])
        for i, (src, dst) in enumerate(((frames, fbuf), (control, cbuf), (gain, line)))
    ]
    for load in loads:
        load.start()
    block = step[0] // 128
    whole_block = pltpu.make_async_copy(
        table.at[:, pl.ds(pl.multiple_of(jnp.minimum(block, 6) * 128, 128), 128)],
        column, sems.at[3],
    )
    last_block = pltpu.make_async_copy(
        table.at[:, pl.ds(896, 104)], tail, sems.at[3]
    )

    @pl.when(block < 7)
    def _():
        whole_block.start()

    @pl.when(block >= 7)
    def _():
        last_block.start()

    loads[0].wait()
    loads[1].wait()
    for m in range(8):
        for f in range(8):
            put(merged, m, f, fbuf[f, m].astype(F32) + cbuf[f, m].astype(F32))
        rows[m] = taken(merged, m).astype(BF)
    facing = jnp.where(odd_band(), 6, 0)
    for i in range(2):
        fold(one.at[i], rows[facing + i])
        fold(two.at[i], rows[6 - facing + i])

    @pl.when(block < 7)
    def _():
        whole_block.wait()
        row[...] = column[...].T

    @pl.when(block >= 7)
    def _():
        last_block.wait()
        row[0:104] = tail[...].T

    vectors[0:1] = row[pl.ds(step[0] % 128, 1), :]
    loads[2].wait()
    vectors[1:2] = line[...].reshape(1, 320)


def inner_kernel(rows, first, vectors, edge, wide1, taps2, taps1, prod):
    embed = vectors[0:1]
    for m in range(8):
        value = rows[m]
        for dy in range(3):
            if 0 <= m - dy < 6:
                tapped(taps1, m - dy, dy, value)
    arrange(wide1, first)
    multiply(prod, taps1, wide1, 6)
    for r in range(6):
        act = silu(combine(prod, r) + embed).astype(BF)
        for dy in range(3):
            if 0 <= r - dy < 4:
                tapped(taps2, r - dy, dy, act)
        if r in (0, 1, 4, 5):
            edge[(0, 1, None, None, 2, 3)[r]] = act


def second_kernel(rows, second, vectors, taps2, keep, give, flat, wide2, prod, normed):
    gain = vectors[1:2]
    arrange(wide2, second)
    multiply(prod, taps2, wide2, 4)
    for y in range(4):
        value = combine(prod, y) + rows[y + 2].astype(F32)
        flat[y] = value
        fold(normed.at[y], layer_norm(value, gain))
    hand_out(in_group(), normed, keep, give)


def outer_kernel(
    reach, one, two, merged, edge, wide1, wide2, vectors, rel_bias, wq, wk, wv, w_out,
    keep, give, flat, weights, bias,
    taps1, taps2, prod, normed, sems,
):
    loads = [
        pltpu.make_async_copy(w, weights.at[i], sems.at[i])
        for i, w in enumerate((wq, wk, wv, w_out))
    ]
    for load in loads:
        load.start()
    me = in_group()
    band = lax.axis_index("band")
    odd = odd_band()
    embed = vectors[0:1]
    gain = vectors[1:2]
    low = [unfold(jnp.where(odd, two[y], one[y])) for y in range(2)]
    high = [unfold(jnp.where(odd, one[y], two[y])) for y in range(2)]
    rows = low + [merged[0], merged[1], merged[6], merged[7]] + high
    starts = (0, 1, 4, 5)
    for m in range(8):
        for r in range(4):
            if 0 <= m - starts[r] < 3:
                tapped(taps1, r, m - starts[r], rows[m])
    multiply(prod, taps1, wide1, 4)
    act = [silu(combine(prod, r) + embed) for r in range(4)]
    act[0] = jnp.where(band == 0, 0.0, act[0])
    act[3] = jnp.where(band == lax.axis_size("band") - 1, 0.0, act[3])
    act = [a.astype(BF) for a in act]
    lines = ((act[0], act[1], edge[0], edge[1]), (edge[2], edge[3], act[2], act[3]))
    for side in range(2):
        for i in range(4):
            for dy in range(3):
                if 0 <= i - dy < 2:
                    tapped(taps2, 2 * side + i - dy, dy, lines[side][i])
    multiply(prod, taps2, wide2, 4)
    for y in range(4):
        value = combine(prod, y) + merged[(0, 1, 6, 7)[y]].astype(F32)
        flat[y] = value
        fold(normed.at[y], layer_norm(value, gain))
    hand_out(me, normed, keep, give)
    bias_table(bias, rel_bias, reach)
    for load in loads:
        load.wait()


def pack_kernel(keep, got, near, far):
    near[0] = keep[0]
    near[1] = got[0]
    far[0] = keep[1]
    far[1] = got[1]


def attend_kernel(
    near, across_x, near_z, across_z, weights, bias,
    out0, out1, out2, out3,
    field, query, key, value, score, prob, back,
):
    me = in_group()
    pixels = field.shape[0]

    for k in range(4):
        block = me ^ k
        own = (near, across_x)[k // 2]
        at = pl.multiple_of(16 + 8 * block, 8)
        field[:, pl.ds(at, 8), :] = unfold(own[k % 2].astype(F32)).reshape(pixels, 8, 320)
        halo = (near_z, across_z)[k // 2]
        at = pl.multiple_of(jnp.where(block >= 2, 8 * block - 16, 48 + 8 * block), 8)
        field[:, pl.ds(at, 8), :] = unfold(halo[k % 2].astype(F32)).reshape(pixels, 8, 320)

    def project(x, i):
        return jnp.dot(x, weights[i], preferred_element_type=F32).astype(BF)

    x = field[...].reshape(pixels * 64, 320).astype(BF)
    key[...] = project(x, 1).reshape(pixels, 64, 320)
    value[...] = project(x, 2).reshape(pixels, 64, 320)
    x = field[:, 16:48, :].reshape(pixels * 32, 320).astype(BF)
    query[...] = project(x, 0).reshape(pixels, 32, 320)

    def heads_at(lanes, base):
        lane = lax.broadcasted_iota(jnp.int32, (4, 1, lanes), 2)
        first = base + 40 * lax.broadcasted_iota(jnp.int32, (4, 1, lanes), 0)
        return ((lane >= first) & (lane < first + 40)).astype(F32).astype(BF)

    spread_low = heads_at(256, 0)
    spread_high = heads_at(192, 32)
    scale = 40.0**-0.5 / math.log(2.0)
    across = (((1,), (1,)), ((), ()))

    def scores(p):
        q = query[p]
        k = key[p]
        low = (q[None, :, 0:256] * spread_low).reshape(128, 256)
        high = (q[None, :, 128:320] * spread_high).reshape(128, 192)
        score[p, :, 0:128] = lax.dot_general(
            k[:, 0:256], low, across, preferred_element_type=F32
        )
        score[p, :, 128:256] = lax.dot_general(
            k[:, 128:320], high, across, preferred_element_type=F32
        )

    def softmax(p):
        s = score[p] * scale + bias[...]
        e = jnp.exp2(s - jnp.max(s, axis=0, keepdims=True))
        prob[p] = (e * (1.0 / jnp.sum(e, axis=0, keepdims=True))).astype(BF)

    def inside(h, lanes, base):
        lane = lax.broadcasted_iota(jnp.int32, (1, lanes), 1) + base
        return (lane >= 40 * h) & (lane < 40 * h + 40)

    def attended(p):
        w = prob[p].T
        v = value[p]
        low = jnp.dot(w[0:128], v[:, 0:256], preferred_element_type=F32)
        high = jnp.dot(w[128:256], v[:, 128:320], preferred_element_type=F32)
        left = low[0:32, 0:128]
        for h in (1, 2, 3):
            left = jnp.where(inside(h, 128, 0), low[32 * h : 32 * h + 32, 0:128], left)
        middle = low[96:128, 128:256]
        for h in (4, 5, 6):
            at = 32 * h - 128
            middle = jnp.where(inside(h, 128, 128), high[at : at + 32, 0:128], middle)
        right = jnp.where(inside(7, 64, 256), high[96:128, 128:192], high[64:96, 128:192])
        att = jnp.concatenate([left, middle, right], axis=1)
        for b in range(4):
            back[b, p] = att[8 * b : 8 * b + 8]

    def each(step):
        def some(i, carry):
            for j in range(16):
                step(i * 16 + j)
            return carry

        lax.fori_loop(0, pixels // 16, some, 0)

    each(scores)
    each(softmax)
    each(attended)
    for k, out in enumerate((out0, out1, out2, out3)):
        fold(out, project(back[me ^ k].reshape(pixels * 8, 320).astype(BF), 3))


def final_kernel(first_row, second_row, *refs):
    a0, a1, a2, a3, flat = refs[:5]
    me = in_group()
    out, total, done, sems = refs[-4:]
    stores = []
    for k, a in enumerate((a0, a1, a2, a3)):
        q = me ^ k
        row = jnp.where(q >= 2, second_row + q - 2, first_row + q)
        value = unfold(a[...].astype(F32)) + flat[q]
        rest = jnp.concatenate([value[:, 256:], jnp.zeros((128, 64), F32)], axis=1)
        for j, part in enumerate((value[:, :128], value[:, 128:256], rest)):
            total[k, j] = part
        for f in range(8):
            for j, width in enumerate((128, 128, 64)):
                part = total[k, j, pl.ds(f, 16, stride=8), :]
                done[k, f, :, j * 128 : j * 128 + width] = part[:, :width]
        store = pltpu.make_async_copy(done.at[k], out.at[:, row], sems.at[k])
        store.start()
        stores.append(store)
    for store in stores:
        store.wait()


def shards(
    frames, control, conv_first, conv_second, time_table, step_index, norm_gain,
    w_query, w_key, w_value, w_out, rel_bias, reach,
):
    count = lax.axis_size("frame")
    bands = lax.axis_size("band")
    planes = count // GROUP
    def swaps(first):
        pairs = [(i, i + 1) for i in range(first, bands - 1, 2)]
        return pairs + [(j, i) for i, j in pairs]

    def plane(i, k):
        return (i & ~3) | ((i & 3) ^ k)

    def beside(i, k):
        turn = 1 if i & 2 else -1
        return (((i >> 2) + turn) % planes) * GROUP + ((i & 3) ^ k)

    def exchange(x, to, k):
        return lax.ppermute(x, "frame", [(i, to(i, k)) for i in range(count)])

    vmem = pl.BlockSpec(memory_space=pltpu.VMEM)
    smem = pl.BlockSpec(memory_space=pltpu.SMEM)
    anywhere = pl.BlockSpec(memory_space=pltpu.HBM)

    def params(mebibytes):
        return pltpu.CompilerParams(vmem_limit_bytes=mebibytes * MIB)
    pair = jax.ShapeDtypeStruct((2, 320, 128), BF)
    chunk = pltpu.VMEM((4, 128, 320), F32)

    def cost(flops):
        return pl.CostEstimate(flops=flops, bytes_accessed=4_000_000, transcendentals=0)

    def stay(*arrays):
        return [pltpu.with_memory_space_constraint(x, pltpu.HBM) for x in arrays]

    def near_by(*arrays):
        return [pltpu.with_memory_space_constraint(x, pltpu.VMEM) for x in arrays]

    rows_scratch = [
        pltpu.VMEM((4, 128, 960), BF),
        pltpu.VMEM((768, 960), F32),
        pltpu.VMEM((4, 320, 128), BF),
    ]
    wide = pltpu.VMEM((960, 960), BF)
    one, two, merged, vectors = pl.pallas_call(
        merge_kernel,
        in_specs=[smem] + [anywhere] * 4,
        out_specs=[vmem] * 4,
        out_shape=[pair, pair, pltpu.VMEM((8, 128, 320), BF), pltpu.VMEM((2, 320), F32)],
        scratch_shapes=[
            pltpu.VMEM((320,), F32),
            pltpu.VMEM((320, 128), F32),
            pltpu.VMEM((320, 104), F32),
            pltpu.VMEM((128, 320), F32),
            pltpu.VMEM((8, 8, 16, 320), BF),
            pltpu.VMEM((8, 8, 16, 320), BF),
            pltpu.VMEM((3, 8, 128, 128), F32),
            pltpu.SemaphoreType.DMA((4,)),
        ],
        compiler_params=params(8),
        name="merge",
    )(step_index, *stay(frames, control, time_table.T, norm_gain))
    one, two, vectors = lax.optimization_barrier((one, two, vectors))
    one = lax.ppermute(one, "band", swaps(1))
    two = lax.ppermute(two, "band", swaps(0))

    first = exchange(conv_first, plane, 1)
    second = exchange(conv_second, plane, 1)
    edge, wide1, taps = pl.pallas_call(
        inner_kernel,
        in_specs=[vmem] * 3,
        out_specs=[vmem] * 3,
        out_shape=[pltpu.VMEM((4, 128, 320), BF), wide, pltpu.VMEM((4, 128, 960), BF)],
        scratch_shapes=[pltpu.VMEM((6, 128, 960), BF), pltpu.VMEM((768, 960), F32)],
        compiler_params=params(10),
        name="inner_rows",
    )(*near_by(merged, first, vectors))
    keep, give, flat_in, wide2 = pl.pallas_call(
        second_kernel,
        in_specs=[vmem] * 4,
        out_specs=[vmem] * 4,
        out_shape=[pair, pair, chunk, wide],
        scratch_shapes=[pltpu.VMEM((512, 960), F32), pltpu.VMEM((4, 320, 128), BF)],
        compiler_params=params(8),
        name="inner_second",
    )(*near_by(merged, second, vectors, taps))

    keep, give, one, two = lax.optimization_barrier((keep, give, one, two))

    def packed(keep, give):
        got = exchange(give, plane, 1)
        return pl.pallas_call(
            pack_kernel,
            in_specs=[vmem] * 2,
            out_specs=[vmem] * 2,
            out_shape=[pair] * 2,
            compiler_params=params(2),
            name="pack",
        )(keep, got)

    def onward(i, k):
        turn = 1 if (i ^ 2) & 2 else -1
        return (((i >> 2) + turn) % planes) * GROUP + (i & 3)

    near_in, far = packed(keep, give)
    x_in = exchange(far, plane, 2)
    z_in = exchange(near_in, beside, 0)
    near_in, edge = lax.optimization_barrier((near_in, edge))

    keep, give, flat_out, weights, bias = pl.pallas_call(
        outer_kernel,
        in_specs=[smem] + [vmem] * 8 + [anywhere] * 4,
        out_specs=[vmem] * 5,
        out_shape=[
            pair, pair, chunk, pltpu.VMEM((4, 320, 320), BF), pltpu.VMEM((64, 256), F32)
        ],
        scratch_shapes=[
            pltpu.VMEM((4, 128, 960), BF),
        ]
        + rows_scratch
        + [pltpu.SemaphoreType.DMA((4,))],
        compiler_params=params(12),
        name="outer_rows",
    )(
        reach, one, two, *near_by(merged, edge, wide1, wide2, vectors), rel_bias,
        *stay(w_query, w_key, w_value, w_out),
    )

    give, x_in, z_in = lax.optimization_barrier((give, x_in, z_in))
    xz_in = exchange(x_in, onward, 0)
    near_out, far = packed(keep, give)
    x_out = exchange(far, plane, 2)
    xz_out = exchange(far, beside, 2)
    z_out = exchange(near_out, beside, 0)

    def attend(fields):
        piece = jax.ShapeDtypeStruct((320, 128), BF)
        outs = pl.pallas_call(
            attend_kernel,
            in_specs=[vmem] * 6,
            out_specs=[vmem] * 4,
            out_shape=[piece] * 4,
            scratch_shapes=[
                pltpu.VMEM((16, 64, 320), F32),
                pltpu.VMEM((16, 32, 320), BF),
                pltpu.VMEM((16, 64, 320), BF),
                pltpu.VMEM((16, 64, 320), BF),
                pltpu.VMEM((16, 64, 256), F32),
                pltpu.VMEM((16, 64, 256), BF),
                pltpu.VMEM((4, 16, 8, 320), F32),
            ],
            compiler_params=params(14),
            name="attend",
        )(*fields, *near_by(weights, bias))
        return [outs[0]] + [exchange(outs[k], plane, k) for k in (2, 3, 1)], outs[0]

    near_out, near_in = lax.optimization_barrier((near_out, near_in))
    (b0, b2, b3, b1), _ = attend((near_in, x_in, z_in, xz_in))
    back_in = [b0, b1, b2, b3]
    (b0, b2, b3, b1), mark = attend((near_out, x_out, z_out, xz_out))
    back_out = [b0, b1, b2, b3]

    def finish(first_row, second_row, back, flat, *before):
        def body(*refs):
            final_kernel(first_row, second_row, *refs)

        return pl.pallas_call(
            body,
            in_specs=[vmem] * 5 + [anywhere] * len(before),
            out_specs=anywhere,
            out_shape=jax.ShapeDtypeStruct(frames.shape, F32),
            input_output_aliases={5: 0} if before else {},
            scratch_shapes=[
                pltpu.VMEM((4, 3, 128, 128), F32),
                pltpu.VMEM((4, 8, 16, 320), F32),
                pltpu.SemaphoreType.DMA((4,)),
            ],
            compiler_params=params(6),
            name="project_out",
        )(*back, *near_by(flat), *before)

    back_in[0], mark = lax.optimization_barrier((back_in[0], mark))
    out = finish(2, 4, back_in, flat_in)
    return finish(0, 6, back_out, flat_out, out)


def solution(mesh):
    tiled = P("frame", "band", None, None)
    return jax.shard_map(
        shards, mesh=mesh, in_specs=(tiled, tiled) + (P(),) * 11, out_specs=tiled, check_vma=False
    )
```
